32 devices in a mesh: dp: 4 (over x, core), mp: 8 (over z, y).
Axes of the slice: x: 2, y: 2, z: 4, core: 2. Of those that a mesh axis runs over, the one named last changes fastest.
Arguments:
- queries: bfloat16 [2048, 1024], P('dp', 'mp'), may hold values from -6 to 6
- keys: bfloat16 [2048, 1024], P('dp', 'mp'), may hold values from -6 to 6
- values: bfloat16 [2048, 1024], P('dp', 'mp'), may hold values from -6 to 6
- w_out: bfloat16 [1024, 6144], P('mp', 'dp'), may hold values from -0.1875 to 0.1875
- cotangent: bfloat16 [2048, 6144], P(('dp', 'mp')), may hold values from -6 to 6
Outputs:
- grad_queries: bfloat16 [2048, 1024], P('dp', 'mp')
- grad_keys: bfloat16 [2048, 1024], P('dp', 'mp')
- grad_values: bfloat16 [2048, 1024], P('dp', 'mp')
- grad_weight: bfloat16 [1024, 6144], P('mp', 'dp')
The draws below stay inside these ranges and needn't reach their ends.
All inputs are finite; a program needn't handle non-finite values.
Results may differ from the reference program's by a relative error of at most 0.022.
Values may be sent and summed in bfloat16 or wider, within the bound.
No kernel may reach another device: no remote copies, remote signals or barrier semaphores. Data moves between devices by JAX's collectives and lax.ppermute only.
A program may use at most 64 MiB of HBM per device.

```python
import jax
import jax.numpy as jnp
from jax import lax

D = 6144
HD = 128
PATCH = 256
HEADS = 8
TOKENS = 2048
N_DP = 4


def draw_queries(key, part):
    key = jax.random.fold_in(key, 11)
    return jnp.clip(jax.random.normal(key, (TOKENS, HEADS * HD), jnp.float32), -4.0, 4.0).astype(jnp.bfloat16)


def draw_keys(key, part):
    key = jax.random.fold_in(key, 23)
    return jnp.clip(jax.random.normal(key, (TOKENS, HEADS * HD), jnp.float32), -4.0, 4.0).astype(jnp.bfloat16)


def spiked(values, key, source, target, shards_of, factor):
    def block_of(dim):
        return (jnp.arange(values.shape[dim]) // (values.shape[dim] // shards_of)).reshape((-1,) + (1,) * (values.ndim - 1 - dim))

    first = jax.random.permutation(key, shards_of)[block_of(target)]
    second = (block_of(target) + shards_of // 2) % shards_of
    return jnp.where((block_of(source) == first) | (block_of(source) == second), factor * values, values)


def steps_of(rng, dims, shards, smallest, largest):
    gain, own = 1.0, jax.random.fold_in(rng, 6)
    for axis_at, blocks in shards:
        heights = jnp.exp(jax.random.uniform(jax.random.fold_in(own, axis_at), (blocks,), jnp.float32, smallest / len(shards), largest / len(shards)))
        gain = gain * jnp.repeat(heights, dims[axis_at] // blocks).reshape([-1 if axis == axis_at else 1 for axis in range(len(dims))])
    return gain


def centred(key, dims, spread, limit, shards=(), dtype=jnp.bfloat16):
    values = spread * jax.random.normal(key, dims, jnp.float32)
    if shards:
        values = values * steps_of(key, dims, shards, -0.22, 0.18)
    return jnp.clip(values, -limit, limit).astype(dtype)


def gaussian_with(stream_key, shape, scale, limit, cuts, heavy, kind=jnp.bfloat16):
    drawn = scale * jax.random.normal(stream_key, shape, jnp.float32)
    if cuts:
        drawn = drawn * steps_of(stream_key, shape, cuts, -0.22, 0.18)
    return jnp.clip(spiked(drawn, jax.random.fold_in(stream_key, 3), *heavy), -limit, limit).astype(kind)


def setup_inputs(seed: int = 0) -> dict:
    key_of = jax.random.split(jax.random.key(seed), 6)
    return {
        "queries": draw_queries(jax.random.fold_in(key_of[5], 71), 0),
        "keys": draw_keys(jax.random.fold_in(key_of[5], 71), 0),
        "values": centred(key_of[2], (TOKENS, HEADS * HD), 1.0, 6.0, ((0, 4), (1, 8))),
        "w_out": centred(key_of[3], (HEADS * HD, D), (HEADS * HD) ** -0.5, 0.1875, ((0, 8), (1, 4))),
        "cotangent": gaussian_with(key_of[4], (TOKENS, D), 1.0, 6.0, ((0, 32),), (0, 1, 32, 2.75)),
    }


def per_image(block):
    queries, keys, values, d_att = block
    scale = HD ** -0.5
    scores = jnp.einsum("qhd,khd->hqk", queries.astype(jnp.float32), keys.astype(jnp.float32)) * scale
    attention = jax.nn.softmax(scores, axis=-1)
    rounded = attention.astype(jnp.bfloat16)
    attended = jnp.einsum("hqk,khd->qhd", rounded.astype(jnp.float32), values.astype(jnp.float32)).astype(jnp.bfloat16)
    dprob = jnp.einsum("qhd,khd->hqk", d_att.astype(jnp.float32), values.astype(jnp.float32))
    delta = jnp.sum(attention * dprob, axis=-1, keepdims=True)
    dscore = (attention * (dprob - delta) * scale).astype(jnp.bfloat16)
    grad_q = jnp.einsum("hqk,khd->qhd", dscore.astype(jnp.float32), keys.astype(jnp.float32)).astype(jnp.bfloat16)
    grad_k = jnp.einsum("hqk,qhd->khd", dscore.astype(jnp.float32), queries.astype(jnp.float32)).astype(jnp.bfloat16)
    grad_v = jnp.einsum("hqk,qhd->khd", rounded.astype(jnp.float32), d_att.astype(jnp.float32)).astype(jnp.bfloat16)
    return attended, grad_q, grad_k, grad_v


def reference(queries, keys, values, w_out, cotangent):
    d_att = jnp.dot(cotangent, w_out.T, preferred_element_type=jnp.float32).astype(jnp.bfloat16)
    shape_four = (TOKENS // PATCH, PATCH, HEADS, HD)
    attended, grad_q, grad_k, grad_v = lax.map(per_image, (queries.reshape(shape_four), keys.reshape(shape_four), values.reshape(shape_four), d_att.reshape(shape_four)))
    flat = (TOKENS, HEADS * HD)
    group_att = attended.reshape(N_DP, TOKENS // N_DP, HEADS * HD)
    group_cot = cotangent.reshape(N_DP, TOKENS // N_DP, D)

    def add_group(total, pair):
        partial_sum = jnp.dot(pair[0].T, pair[1], preferred_element_type=jnp.float32)
        partial_sum = lax.optimization_barrier(partial_sum.astype(jnp.bfloat16)).astype(jnp.float32)
        return total + partial_sum, None

    total, unused = lax.scan(add_group, jnp.zeros((HEADS * HD, D), jnp.float32), (group_att, group_cot))
    return grad_q.reshape(flat), grad_k.reshape(flat), grad_v.reshape(flat), total.astype(jnp.bfloat16)
```

```python
import functools

import jax
import jax.numpy as jnp
from jax import lax
from jax.experimental import pallas as pl
from jax.experimental.pallas import tpu as pltpu
from jax.sharding import PartitionSpec as P

HD = 128
PATCH = 256
AXES = ("dp", "mp")
ANY = pl.BlockSpec(memory_space=pl.ANY)
VMEM = pl.BlockSpec(memory_space=pltpu.VMEM)
F32 = jnp.float32
BF16 = jnp.bfloat16


def forward_attention(queries, keys, values):
    images = queries.shape[0] // PATCH
    heads_here = queries.shape[1] // HD
    shape_four = (images, PATCH, heads_here, HD)
    scale = HD ** (-0.5)
    query_four = queries.reshape(shape_four)
    key_four = keys.reshape(shape_four)
    value_four = values.reshape(shape_four)
    scores = (
        jnp.einsum("iqhd,ikhd->ihqk", query_four, key_four, preferred_element_type=jnp.float32)
        * scale
    )
    attention = jax.nn.softmax(scores, axis=-1)
    rounded = attention.astype(jnp.bfloat16)
    attended = jnp.einsum(
        "ihqk,ikhd->iqhd", rounded, value_four, preferred_element_type=jnp.float32
    ).astype(jnp.bfloat16)
    return (attended.reshape(queries.shape), attention, rounded)


def backward_attention(queries, keys, values, d_att, attention, rounded):
    images = queries.shape[0] // PATCH
    heads_here = queries.shape[1] // HD
    shape_four = (images, PATCH, heads_here, HD)
    scale = HD ** (-0.5)
    query_four = queries.reshape(shape_four)
    key_four = keys.reshape(shape_four)
    value_four = values.reshape(shape_four)
    grad_four = d_att.reshape(shape_four)
    dprob = jnp.einsum("iqhd,ikhd->ihqk", grad_four, value_four, preferred_element_type=jnp.float32)
    delta = jnp.sum(attention * dprob, axis=-1, keepdims=True)
    dscore = (attention * (dprob - delta) * scale).astype(jnp.bfloat16)
    grad_q = jnp.einsum(
        "ihqk,ikhd->iqhd", dscore, key_four, preferred_element_type=jnp.float32
    ).astype(jnp.bfloat16)
    grad_k = jnp.einsum(
        "ihqk,iqhd->ikhd", dscore, query_four, preferred_element_type=jnp.float32
    ).astype(jnp.bfloat16)
    grad_v = jnp.einsum(
        "ihqk,iqhd->ikhd", rounded, grad_four, preferred_element_type=jnp.float32
    ).astype(jnp.bfloat16)
    return (
        grad_q.reshape(queries.shape),
        grad_k.reshape(queries.shape),
        grad_v.reshape(queries.shape),
    )


def on_device(queries, keys, values, w_out, cotangent):
    attended, attention, rounded = forward_attention(queries, keys, values)
    cot_full = lax.all_gather(cotangent, "mp", axis=0, tiled=True)
    d_full = lax.dot_general(
        cot_full,
        lax.all_gather(w_out, "dp", axis=1, tiled=True),
        (((1,), (1,)), ((), ())),
        preferred_element_type=jnp.float32,
    )
    grad_part = lax.dot_general(
        attended, cot_full, (((0,), (0,)), ((), ())), preferred_element_type=jnp.float32
    )
    d_att = d_full.astype(jnp.bfloat16)
    grad_q, grad_k, grad_v = backward_attention(queries, keys, values, d_att, attention, rounded)
    grad_weight = lax.psum_scatter(
        grad_part.astype(jnp.bfloat16), "dp", scatter_dimension=1, tiled=True
    )
    return (grad_q, grad_k, grad_v, grad_weight)


def flip(x=0, c=0, z1=0, z0=0, y=0):
    mask = (x * 2 + c) * 8 + z1 * 4 + z0 * 2 + y
    return [(i, i ^ mask) for i in range(32)]


def send(value, **bits):
    return lax.ppermute(value, AXES, flip(**bits))


def place():
    dp, mp = lax.axis_index("dp"), lax.axis_index("mp")
    return {"x": dp // 2, "c": dp % 2, "z1": mp // 4, "z0": (mp // 2) % 2, "y": mp % 2}


def aligned(index, unit):
    return pl.multiple_of(index * unit, unit)


def pack_kernel(cuts, cot, *rest):
    outs, sems = rest[:-1], rest[-1]
    x = place()["x"]
    quarter = cot.shape[1] // 4
    copies = []
    for n, (low, high) in enumerate(cuts):
        for other in range(2):
            half = 1 - x if other else x
            for c in range(2):
                start = pl.multiple_of(half * (2 * quarter) + (c * quarter + low), 128)
                width = high - low
                copies.append(
                    pltpu.make_async_copy(
                        cot.at[:, pl.ds(start, width)],
                        outs[2 * n + other].at[:, pl.ds(c * width, width)],
                        sems.at[len(copies)],
                    )
                )
    for copy in copies:
        copy.start()
    for copy in copies:
        copy.wait()


def pack(cot, cuts):
    shapes = []
    for low, high in cuts:
        shapes += [jax.ShapeDtypeStruct((cot.shape[0], 2 * (high - low)), cot.dtype)] * 2
    return pl.pallas_call(
        functools.partial(pack_kernel, cuts),
        out_shape=shapes,
        in_specs=[ANY],
        out_specs=[ANY] * len(shapes),
        scratch_shapes=[pltpu.SemaphoreType.DMA((4 * len(cuts),))],
        cost_estimate=pl.CostEstimate(flops=0, bytes_accessed=2 * cot.size * 2, transcendentals=0),
        name="pack",
    )(cot)


def dot(a, b, over):
    return lax.dot_general(a, b, ((over[0], over[1]), ((), ())), preferred_element_type=F32)


def forward_kernel(q, k, v, probs, mine, others, held):
    z0 = place()["z0"]
    half = PATCH // 2
    for i in range(q.shape[0] // PATCH):
        rows = pl.ds(i * PATCH, PATCH)
        scores = dot(k[rows], q[rows], ((1,), (1,))) * (HD**-0.5)
        top = jnp.max(scores, axis=0, keepdims=True)
        raised = jnp.exp(scores - top)
        attention = raised / jnp.sum(raised, axis=0, keepdims=True)
        probs[i] = attention
        held[...] = dot(attention.astype(BF16), v[rows], ((0,), (0,))).astype(BF16)
        mine[pl.ds(i * half, half)] = held[pl.ds(aligned(z0, half), half)]
        others[pl.ds(i * half, half)] = held[pl.ds(aligned(1 - z0, half), half)]


def forward(q, k, v):
    images = q.shape[0] // PATCH
    half = jax.ShapeDtypeStruct((q.shape[0] // 2, HD), BF16)
    return pl.pallas_call(
        forward_kernel,
        out_shape=[jax.ShapeDtypeStruct((images, PATCH, PATCH), F32), half, half],
        in_specs=[VMEM] * 3,
        out_specs=[VMEM] * 3,
        scratch_shapes=[pltpu.VMEM((PATCH, HD), BF16)],
        cost_estimate=pl.CostEstimate(
            flops=4 * images * PATCH * PATCH * HD,
            bytes_accessed=1 << 20,
            transcendentals=images * PATCH * PATCH,
        ),
        name="forward",
    )(q, k, v)


def backward_kernel(q, k, v, probs, own, from_x, from_z, from_xz, gq, gk, gv, held):
    z0 = place()["z0"]
    half = PATCH // 2
    mine = (own[...] + from_x[...].astype(F32)).astype(BF16)
    others = (from_z[...].astype(F32) + from_xz[...].astype(F32)).astype(BF16)
    for i in range(q.shape[0] // PATCH):
        held[i, pl.ds(aligned(z0, half), half)] = mine[i * half : (i + 1) * half]
        held[i, pl.ds(aligned(1 - z0, half), half)] = others[i * half : (i + 1) * half]
    for i in range(q.shape[0] // PATCH):
        rows = pl.ds(i * PATCH, PATCH)
        attention, d_att = probs[i], held[i]
        dprob = dot(v[rows], d_att, ((1,), (1,)))
        delta = jnp.sum(attention * dprob, axis=0, keepdims=True)
        dscore = (attention * (dprob - delta) * (HD**-0.5)).astype(BF16)
        gv[rows] = dot(attention.astype(BF16), d_att, ((1,), (0,))).astype(BF16)
        gk[rows] = dot(dscore, q[rows], ((1,), (0,))).astype(BF16)
        gq[rows] = dot(dscore, k[rows], ((0,), (0,))).astype(BF16)


def backward(q, k, v, probs, own, from_x, from_z, from_xz):
    images = q.shape[0] // PATCH
    return pl.pallas_call(
        backward_kernel,
        out_shape=[jax.ShapeDtypeStruct(q.shape, BF16)] * 3,
        in_specs=[VMEM] * 8,
        out_specs=[VMEM] * 3,
        scratch_shapes=[pltpu.VMEM((images, PATCH, HD), BF16)],
        cost_estimate=pl.CostEstimate(
            flops=8 * images * PATCH * PATCH * HD, bytes_accessed=2 << 20, transcendentals=0
        ),
        name="backward",
    )(q, k, v, probs, own, from_x, from_z, from_xz)


def products_kernel(low, high, first, last, *refs):
    refs = list(refs)
    blocks = [refs.pop(0) for _ in range(8)]
    w_refs = [refs.pop(0) for _ in range(4)]
    att = [refs.pop(0) for _ in range(4)]
    before = None if first else refs.pop(0)
    keep, give = refs.pop(0), refs.pop(0)
    d_refs = [refs.pop(0) for _ in range(4 if last else 1)]
    c_held, w_held, g_held, sems = refs
    at = place()
    width = high - low
    copies = []
    for n, block in enumerate(blocks):
        group, z1, y = n // 4, (n // 2) % 2, n % 2
        z1 = 1 - at["z1"] if z1 else at["z1"]
        y = 1 - at["y"] if y else at["y"]
        row = pl.multiple_of(group * 256 + z1 * 128 + y * 64, 64)
        copies.append(pltpu.make_async_copy(block, c_held.at[pl.ds(row, 64)], sems.at[n]))
    for n, w in enumerate(w_refs):
        c = 1 - at["c"] if n // 2 else at["c"]
        copies.append(
            pltpu.make_async_copy(
                w.at[:, pl.ds(low, width)],
                w_held.at[pl.ds((n % 2) * HD, HD), pl.ds(pl.multiple_of(c * width, 128), width)],
                sems.at[8 + n],
            )
        )
    for copy in copies:
        copy.start()
    attended = jnp.concatenate(
        [
            jnp.concatenate([att[0][...], att[2][...]], axis=1),
            jnp.concatenate([att[1][...], att[3][...]], axis=1),
        ],
        axis=0,
    )
    for copy in copies:
        copy.wait()
    g_held[...] = dot(attended, c_held[...], ((0,), (0,)))
    keep[...] = g_held[:, pl.ds(pl.multiple_of(at["c"] * width, 128), width)]
    give[...] = g_held[:, pl.ds(pl.multiple_of((1 - at["c"]) * width, 128), width)].astype(BF16)
    d = dot(c_held[...], w_held[...], ((1,), (1,)))
    if not first:
        d = d + before[...]
    if not last:
        d_refs[0][...] = d
    else:
        d_refs[0][...] = d[:256, :HD]
        d_refs[1][...] = d[256:, :HD].astype(BF16)
        d_refs[2][...] = d[:256, HD:].astype(BF16)
        d_refs[3][...] = d[256:, HD:].astype(BF16)


def products(low, high, blocks, w_all, att, before, last):
    width = high - low
    first = before is None
    out = [
        jax.ShapeDtypeStruct((2 * HD, width), F32),
        jax.ShapeDtypeStruct((2 * HD, width), BF16),
    ]
    if last:
        out.append(jax.ShapeDtypeStruct((256, HD), F32))
        out += [jax.ShapeDtypeStruct((256, HD), BF16)] * 3
    else:
        out.append(jax.ShapeDtypeStruct((512, 2 * HD), F32))
    extra = [] if first else [before]
    return pl.pallas_call(
        functools.partial(products_kernel, low, high, first, last),
        out_shape=out,
        in_specs=[ANY] * 12 + [VMEM] * (4 + len(extra)),
        out_specs=[VMEM] * len(out),
        scratch_shapes=[
            pltpu.VMEM((512, 2 * width), BF16),
            pltpu.VMEM((2 * HD, 2 * width), BF16),
            pltpu.VMEM((2 * HD, 2 * width), F32),
            pltpu.SemaphoreType.DMA((12,)),
        ],
        cost_estimate=pl.CostEstimate(
            flops=4 * 512 * 2 * HD * 2 * width,
            bytes_accessed=512 * 2 * width * 2 + 2 * HD * 2 * width * 6,
            transcendentals=0,
        ),
        name="products",
    )(*blocks, *w_all, *att, *extra)


CUTS = ((0, 1024), (1024, 1536))


def on_device_4x8(queries, keys, values, w_out, cotangent):
    packed = pack(cotangent, CUTS)
    gathered = []
    for n in range(len(CUTS)):
        m, o = packed[2 * n], packed[2 * n + 1]
        za, zb = send(m, z1=1), send(o, x=1, z1=1)
        ya, xo, yb = send(m, y=1), send(o, x=1), send(o, x=1, y=1)
        gathered.append([m, ya, za, send(za, y=1), xo, yb, zb, send(zb, y=1)])
    w_pair = send(w_out, z0=1)
    w_all = [w_out, w_pair, send(w_out, c=1), send(w_pair, c=1)]
    probs, mine, others = forward(queries, keys, values)
    att = [mine, send(mine, x=1), send(others, z0=1), send(others, x=1, z0=1)]
    before, parts = None, []
    for n, (low, high) in enumerate(CUTS):
        last = n == len(CUTS) - 1
        keep, give, *d = products(low, high, gathered[n], w_all, att, before, last)
        before = d[0]
        total = keep + send(give, c=1).astype(F32)
        pair = send(total[HD:].astype(BF16), z0=1)
        parts.append((total[:HD] + pair.astype(F32)).astype(BF16))
    own, to_x, to_z, to_xz = d
    grad_q, grad_k, grad_v = backward(
        queries, keys, values, probs, own, send(to_x, x=1), send(to_z, z0=1), send(to_xz, x=1, z0=1)
    )
    return grad_q, grad_k, grad_v, jnp.concatenate(parts, axis=1)


def solution(mesh):
    in_specs = (P("dp", "mp"), P("dp", "mp"), P("dp", "mp"), P("mp", "dp"), P(("dp", "mp"), None))
    out_specs = (P("dp", "mp"), P("dp", "mp"), P("dp", "mp"), P("mp", "dp"))
    small = mesh.shape["dp"] == 4 and mesh.shape["mp"] == 8
    return jax.shard_map(
        on_device_4x8 if small else on_device,
        mesh=mesh,
        in_specs=in_specs,
        out_specs=out_specs,
        check_vma=False,
    )
```

```python
import functools

import jax
import jax.numpy as jnp
from jax import lax
from jax.experimental import pallas as pl
from jax.experimental.pallas import tpu as pltpu
from jax.sharding import PartitionSpec as P

HD = 128
PATCH = 256
AXES = ("dp", "mp")
ANY = pl.BlockSpec(memory_space=pl.ANY)
VMEM = pl.BlockSpec(memory_space=pltpu.VMEM)
F32 = jnp.float32
BF16 = jnp.bfloat16


def forward_attention(queries, keys, values):
    images = queries.shape[0] // PATCH
    heads_here = queries.shape[1] // HD
    shape_four = (images, PATCH, heads_here, HD)
    scale = HD ** (-0.5)
    query_four = queries.reshape(shape_four)
    key_four = keys.reshape(shape_four)
    value_four = values.reshape(shape_four)
    scores = (
        jnp.einsum("iqhd,ikhd->ihqk", query_four, key_four, preferred_element_type=jnp.float32)
        * scale
    )
    attention = jax.nn.softmax(scores, axis=-1)
    rounded = attention.astype(jnp.bfloat16)
    attended = jnp.einsum(
        "ihqk,ikhd->iqhd", rounded, value_four, preferred_element_type=jnp.float32
    ).astype(jnp.bfloat16)
    return (attended.reshape(queries.shape), attention, rounded)


def backward_attention(queries, keys, values, d_att, attention, rounded):
    images = queries.shape[0] // PATCH
    heads_here = queries.shape[1] // HD
    shape_four = (images, PATCH, heads_here, HD)
    scale = HD ** (-0.5)
    query_four = queries.reshape(shape_four)
    key_four = keys.reshape(shape_four)
    value_four = values.reshape(shape_four)
    grad_four = d_att.reshape(shape_four)
    dprob = jnp.einsum("iqhd,ikhd->ihqk", grad_four, value_four, preferred_element_type=jnp.float32)
    delta = jnp.sum(attention * dprob, axis=-1, keepdims=True)
    dscore = (attention * (dprob - delta) * scale).astype(jnp.bfloat16)
    grad_q = jnp.einsum(
        "ihqk,ikhd->iqhd", dscore, key_four, preferred_element_type=jnp.float32
    ).astype(jnp.bfloat16)
    grad_k = jnp.einsum(
        "ihqk,iqhd->ikhd", dscore, query_four, preferred_element_type=jnp.float32
    ).astype(jnp.bfloat16)
    grad_v = jnp.einsum(
        "ihqk,iqhd->ikhd", rounded, grad_four, preferred_element_type=jnp.float32
    ).astype(jnp.bfloat16)
    return (
        grad_q.reshape(queries.shape),
        grad_k.reshape(queries.shape),
        grad_v.reshape(queries.shape),
    )


def on_device(queries, keys, values, w_out, cotangent):
    attended, attention, rounded = forward_attention(queries, keys, values)
    cot_full = lax.all_gather(cotangent, "mp", axis=0, tiled=True)
    d_full = lax.dot_general(
        cot_full,
        lax.all_gather(w_out, "dp", axis=1, tiled=True),
        (((1,), (1,)), ((), ())),
        preferred_element_type=jnp.float32,
    )
    grad_part = lax.dot_general(
        attended, cot_full, (((0,), (0,)), ((), ())), preferred_element_type=jnp.float32
    )
    d_att = d_full.astype(jnp.bfloat16)
    grad_q, grad_k, grad_v = backward_attention(queries, keys, values, d_att, attention, rounded)
    grad_weight = lax.psum_scatter(
        grad_part.astype(jnp.bfloat16), "dp", scatter_dimension=1, tiled=True
    )
    return (grad_q, grad_k, grad_v, grad_weight)


def flip(x=0, c=0, z1=0, z0=0, y=0):
    mask = (x * 2 + c) * 8 + z1 * 4 + z0 * 2 + y
    return [(i, i ^ mask) for i in range(32)]


def send(value, **bits):
    return lax.ppermute(value, AXES, flip(**bits))


def place():
    dp, mp = lax.axis_index("dp"), lax.axis_index("mp")
    return {"x": dp // 2, "c": dp % 2, "z1": mp // 4, "z0": (mp // 2) % 2, "y": mp % 2}


def aligned(index, unit):
    return pl.multiple_of(index * unit, unit)


def pack_kernel(cuts, cot, *outs):
    x = place()["x"]
    quarter = cot.shape[1] // 4
    for n, (low, high) in enumerate(cuts):
        width = high - low
        for other in range(2):
            half = 1 - x if other else x
            for c in range(2):
                start = pl.multiple_of(half * (2 * quarter) + (c * quarter + low), 128)
                outs[2 * n + other][:, c * width : (c + 1) * width] = cot[:, pl.ds(start, width)]


def pack(cot, cuts):
    shapes = []
    for low, high in cuts:
        shapes += [jax.ShapeDtypeStruct((cot.shape[0], 2 * (high - low)), cot.dtype)] * 2
    return pl.pallas_call(
        functools.partial(pack_kernel, cuts),
        out_shape=shapes,
        in_specs=[VMEM],
        out_specs=[VMEM] * len(shapes),
        cost_estimate=pl.CostEstimate(flops=0, bytes_accessed=2 * cot.size * 2, transcendentals=0),
        name="pack",
    )(cot)


def dot(a, b, over):
    return lax.dot_general(a, b, ((over[0], over[1]), ((), ())), preferred_element_type=F32)


def forward_kernel(q, k, v, probs, mine, others, held):
    z0 = place()["z0"]
    half = PATCH // 2
    for i in range(q.shape[0] // PATCH):
        rows = pl.ds(i * PATCH, PATCH)
        scores = dot(k[rows], q[rows], ((1,), (1,))) * (HD**-0.5)
        top = jnp.max(scores, axis=0, keepdims=True)
        raised = jnp.exp(scores - top)
        attention = raised / jnp.sum(raised, axis=0, keepdims=True)
        probs[i] = attention
        held[...] = dot(attention.astype(BF16), v[rows], ((0,), (0,))).astype(BF16)
        mine[pl.ds(i * half, half)] = held[pl.ds(aligned(z0, half), half)]
        others[pl.ds(i * half, half)] = held[pl.ds(aligned(1 - z0, half), half)]


def forward(q, k, v):
    images = q.shape[0] // PATCH
    half = jax.ShapeDtypeStruct((q.shape[0] // 2, HD), BF16)
    return pl.pallas_call(
        forward_kernel,
        out_shape=[jax.ShapeDtypeStruct((images, PATCH, PATCH), F32), half, half],
        in_specs=[VMEM] * 3,
        out_specs=[VMEM] * 3,
        scratch_shapes=[pltpu.VMEM((PATCH, HD), BF16)],
        cost_estimate=pl.CostEstimate(
            flops=4 * images * PATCH * PATCH * HD,
            bytes_accessed=1 << 20,
            transcendentals=images * PATCH * PATCH,
        ),
        name="forward",
    )(q, k, v)


def backward_kernel(q, k, v, probs, own, from_x, from_z, from_xz, gq, gk, gv, held):
    z0 = place()["z0"]
    half = PATCH // 2
    mine = (own[...] + from_x[...].astype(F32)).astype(BF16)
    others = (from_z[...].astype(F32) + from_xz[...].astype(F32)).astype(BF16)
    for i in range(q.shape[0] // PATCH):
        held[i, pl.ds(aligned(z0, half), half)] = mine[i * half : (i + 1) * half]
        held[i, pl.ds(aligned(1 - z0, half), half)] = others[i * half : (i + 1) * half]
    for i in range(q.shape[0] // PATCH):
        rows = pl.ds(i * PATCH, PATCH)
        attention, d_att = probs[i], held[i]
        dprob = dot(v[rows], d_att, ((1,), (1,)))
        delta = jnp.sum(attention * dprob, axis=0, keepdims=True)
        dscore = (attention * (dprob - delta) * (HD**-0.5)).astype(BF16)
        gv[rows] = dot(attention.astype(BF16), d_att, ((1,), (0,))).astype(BF16)
        gk[rows] = dot(dscore, q[rows], ((1,), (0,))).astype(BF16)
        gq[rows] = dot(dscore, k[rows], ((0,), (0,))).astype(BF16)


def backward(q, k, v, probs, own, from_x, from_z, from_xz):
    images = q.shape[0] // PATCH
    return pl.pallas_call(
        backward_kernel,
        out_shape=[jax.ShapeDtypeStruct(q.shape, BF16)] * 3,
        in_specs=[VMEM] * 8,
        out_specs=[VMEM] * 3,
        scratch_shapes=[pltpu.VMEM((images, PATCH, HD), BF16)],
        cost_estimate=pl.CostEstimate(
            flops=8 * images * PATCH * PATCH * HD, bytes_accessed=2 << 20, transcendentals=0
        ),
        name="backward",
    )(q, k, v, probs, own, from_x, from_z, from_xz)


def products_kernel(low, high, first, last, pieces, *refs):
    refs = list(refs)
    cots = [refs.pop(0) for _ in range(1 + max(ref for ref, _ in pieces))]
    w_own, w_core = refs.pop(0), refs.pop(0)
    att_own, att_x = refs.pop(0), refs.pop(0)
    before = None if first else refs.pop(0)
    keep, give = refs.pop(0), refs.pop(0)
    d_refs = refs
    at = place()
    width = high - low
    tile = min(width, 512)
    rows = []
    for n in range(4):
        z1 = 1 - at["z1"] if n // 2 else at["z1"]
        y = 1 - at["y"] if n % 2 else at["y"]
        rows.append(pl.multiple_of(z1 * 128 + y * 64, 64))
    attended = jnp.concatenate(
        [
            jnp.concatenate([att[pl.ds(row, 64)], att[pl.ds(256 + row, 64)]], axis=1)
            for att in (att_own, att_x)
            for row in rows
        ],
        axis=0,
    )
    turned = attended.T
    d = None if first else before[...]
    for other in (1, 0):
        c = 1 - at["c"] if other else at["c"]
        w_ref = w_core if other else w_own
        for start in range(0, width, tile):
            columns = pl.ds(pl.multiple_of(c * width + start, 128), tile)
            cot = jnp.concatenate(
                [cots[ref][row : row + 64, columns] for ref, row in pieces], axis=0
            )
            share = dot(turned, cot, ((1,), (0,)))
            if other:
                give[:, start : start + tile] = share.astype(BF16)
            else:
                keep[:, start : start + tile] = share
            part = dot(cot, w_ref[:, low + start : low + start + tile], ((1,), (1,)))
            d = part if d is None else d + part
    if not last:
        d_refs[0][...] = d
    else:
        for n, row in enumerate(rows):
            for g in range(2):
                share = d[(4 * g + n) * 64 : (4 * g + n + 1) * 64]
                d_refs[g][pl.ds(row, 64)] = share[:, :HD].astype(d_refs[g].dtype)
                d_refs[2 + g][pl.ds(row, 64)] = share[:, HD:].astype(BF16)


def products(low, high, pieces, cots, w_all, att, before, last):
    width = high - low
    first = before is None
    out = [
        jax.ShapeDtypeStruct((2 * HD, width), F32),
        jax.ShapeDtypeStruct((2 * HD, width), BF16),
    ]
    if last:
        out.append(jax.ShapeDtypeStruct((256, HD), F32))
        out += [jax.ShapeDtypeStruct((256, HD), BF16)] * 3
    else:
        out.append(jax.ShapeDtypeStruct((512, 2 * HD), F32))
    extra = [] if first else [before]
    return pl.pallas_call(
        functools.partial(products_kernel, low, high, first, last, pieces),
        out_shape=out,
        in_specs=[VMEM] * (len(cots) + 4 + len(extra)),
        out_specs=[VMEM] * len(out),
        cost_estimate=pl.CostEstimate(
            flops=4 * 512 * 2 * HD * 2 * width,
            bytes_accessed=512 * 2 * width * 2 + 2 * HD * 2 * width * 6,
            transcendentals=0,
        ),
        name="products",
    )(*cots, *w_all, *att, *extra)


def after(value, *others):
    return lax.optimization_barrier((value, *others))[0]


CUTS = ((0, 1024), (1024, 1536))


def on_device_4x8(queries, keys, values, w_out, cotangent):
    m1, o1, m2, o2 = pack(cotangent, CUTS)
    za1, x1 = send(m1, z1=1), send(o1, x=1)
    w_z = send(w_out, z0=1)
    zb1 = send(x1, z1=1)
    y1 = send(jnp.concatenate([m1, x1]), y=1)
    x2 = send(after(o2, x1), x=1)
    sa1 = send(za1, y=1)
    mx2 = jnp.concatenate([m2, x2])
    z2 = send(after(mx2, za1), z1=1)
    y2 = send(after(mx2, y1), y=1)
    sb1 = send(zb1, y=1)
    s2 = send(after(z2, y2), y=1)
    w_own = jnp.concatenate([w_out, w_z])
    w_all = [w_own, send(after(w_own, za1), c=1)]
    q, k, v, _ = lax.optimization_barrier((queries, keys, values, x1))
    probs, mine, others = forward(q, k, v)
    att = jnp.concatenate([mine, send(after(others, y1), z0=1)])
    att = [att, send(att, x=1)]
    inputs = [
        ([m1, x1, y1, za1, sa1, zb1, sb1], [(0, 0), (2, 0), (3, 0), (4, 0), (1, 0), (2, 64), (5, 0), (6, 0)]),
        ([mx2, y2, z2, s2], [(0, 0), (1, 0), (2, 0), (3, 0), (0, 64), (1, 64), (2, 64), (3, 64)]),
    ]
    before, parts = None, []
    for n, (low, high) in enumerate(CUTS):
        last = n == len(CUTS) - 1
        cots, pieces = inputs[n]
        keep, give, *d = products(low, high, pieces, cots, w_all, att, before, last)
        total = keep + send(give, c=1).astype(F32)
        to_pair = total[HD:].astype(BF16)
        pair = send(to_pair, z0=1)
        before = after(d[0], to_pair)
        parts.append((total[:HD] + pair.astype(F32)).astype(BF16))
    own, to_x, to_z, to_xz = d
    grad_q, grad_k, grad_v = backward(
        q, k, v, probs, own, send(to_x, x=1), send(to_z, z0=1), send(to_xz, x=1, z0=1)
    )
    return grad_q, grad_k, grad_v, jnp.concatenate(parts, axis=1)


def solution(mesh):
    in_specs = (P("dp", "mp"), P("dp", "mp"), P("dp", "mp"), P("mp", "dp"), P(("dp", "mp"), None))
    out_specs = (P("dp", "mp"), P("dp", "mp"), P("dp", "mp"), P("mp", "dp"))
    small = mesh.shape["dp"] == 4 and mesh.shape["mp"] == 8
    return jax.shard_map(
        on_device_4x8 if small else on_device,
        mesh=mesh,
        in_specs=in_specs,
        out_specs=out_specs,
        check_vma=False,
    )
```

```python
import functools

import jax
import jax.numpy as jnp
from jax import lax
from jax.experimental import pallas as pl
from jax.experimental.pallas import tpu as pltpu
from jax.sharding import PartitionSpec as P

HD = 128
PATCH = 256
AXES = ("dp", "mp")
ANY = pl.BlockSpec(memory_space=pl.ANY)
VMEM = pl.BlockSpec(memory_space=pltpu.VMEM)
F32 = jnp.float32
COST = pl.CostEstimate(flops=2 * 10**10, bytes_accessed=1 << 20, transcendentals=0)
BF16 = jnp.bfloat16


def forward_attention(queries, keys, values):
    images = queries.shape[0] // PATCH
    heads_here = queries.shape[1] // HD
    shape_four = (images, PATCH, heads_here, HD)
    scale = HD ** (-0.5)
    query_four = queries.reshape(shape_four)
    key_four = keys.reshape(shape_four)
    value_four = values.reshape(shape_four)
    scores = (
        jnp.einsum("iqhd,ikhd->ihqk", query_four, key_four, preferred_element_type=jnp.float32)
        * scale
    )
    attention = jax.nn.softmax(scores, axis=-1)
    rounded = attention.astype(jnp.bfloat16)
    attended = jnp.einsum(
        "ihqk,ikhd->iqhd", rounded, value_four, preferred_element_type=jnp.float32
    ).astype(jnp.bfloat16)
    return (attended.reshape(queries.shape), attention, rounded)


def backward_attention(queries, keys, values, d_att, attention, rounded):
    images = queries.shape[0] // PATCH
    heads_here = queries.shape[1] // HD
    shape_four = (images, PATCH, heads_here, HD)
    scale = HD ** (-0.5)
    query_four = queries.reshape(shape_four)
    key_four = keys.reshape(shape_four)
    value_four = values.reshape(shape_four)
    grad_four = d_att.reshape(shape_four)
    dprob = jnp.einsum("iqhd,ikhd->ihqk", grad_four, value_four, preferred_element_type=jnp.float32)
    delta = jnp.sum(attention * dprob, axis=-1, keepdims=True)
    dscore = (attention * (dprob - delta) * scale).astype(jnp.bfloat16)
    grad_q = jnp.einsum(
        "ihqk,ikhd->iqhd", dscore, key_four, preferred_element_type=jnp.float32
    ).astype(jnp.bfloat16)
    grad_k = jnp.einsum(
        "ihqk,iqhd->ikhd", dscore, query_four, preferred_element_type=jnp.float32
    ).astype(jnp.bfloat16)
    grad_v = jnp.einsum(
        "ihqk,iqhd->ikhd", rounded, grad_four, preferred_element_type=jnp.float32
    ).astype(jnp.bfloat16)
    return (
        grad_q.reshape(queries.shape),
        grad_k.reshape(queries.shape),
        grad_v.reshape(queries.shape),
    )


def on_device(queries, keys, values, w_out, cotangent):
    attended, attention, rounded = forward_attention(queries, keys, values)
    cot_full = lax.all_gather(cotangent, "mp", axis=0, tiled=True)
    d_full = lax.dot_general(
        cot_full,
        lax.all_gather(w_out, "dp", axis=1, tiled=True),
        (((1,), (1,)), ((), ())),
        preferred_element_type=jnp.float32,
    )
    grad_part = lax.dot_general(
        attended, cot_full, (((0,), (0,)), ((), ())), preferred_element_type=jnp.float32
    )
    d_att = d_full.astype(jnp.bfloat16)
    grad_q, grad_k, grad_v = backward_attention(queries, keys, values, d_att, attention, rounded)
    grad_weight = lax.psum_scatter(
        grad_part.astype(jnp.bfloat16), "dp", scatter_dimension=1, tiled=True
    )
    return (grad_q, grad_k, grad_v, grad_weight)


def flip(x=0, c=0, z1=0, z0=0, y=0):
    mask = (x * 2 + c) * 8 + z1 * 4 + z0 * 2 + y
    return [(i, i ^ mask) for i in range(32)]


def send(value, **bits):
    return lax.ppermute(value, AXES, flip(**bits))


def place():
    dp, mp = lax.axis_index("dp"), lax.axis_index("mp")
    return {"x": dp // 2, "c": dp % 2, "z1": mp // 4, "z0": (mp // 2) % 2, "y": mp % 2}


def aligned(index, unit):
    return pl.multiple_of(index * unit, unit)


def pack_kernel(cuts, cot, *outs):
    x = place()["x"]
    quarter = cot.shape[1] // 4
    for n, (low, high) in enumerate(cuts):
        width = high - low
        for other in range(2):
            half = 1 - x if other else x
            for c in range(2):
                start = pl.multiple_of(half * (2 * quarter) + (c * quarter + low), 128)
                outs[2 * n + other][:, c * width : (c + 1) * width] = cot[:, pl.ds(start, width)]


def pack(cot, cuts):
    shapes = []
    for low, high in cuts:
        shapes += [jax.ShapeDtypeStruct((cot.shape[0], 2 * (high - low)), cot.dtype)] * 2
    return pl.pallas_call(
        functools.partial(pack_kernel, cuts),
        out_shape=shapes,
        in_specs=[VMEM],
        out_specs=[VMEM] * len(shapes),
        cost_estimate=COST,
        name="pack",
    )(cot)


def dot(a, b, over):
    return lax.dot_general(a, b, ((over[0], over[1]), ((), ())), preferred_element_type=F32)


def forward_kernel(q, k, v, probs, mine, others, held):
    z0 = place()["z0"]
    half = PATCH // 2
    for i in range(q.shape[0] // PATCH):
        rows = pl.ds(i * PATCH, PATCH)
        scores = dot(k[rows], q[rows], ((1,), (1,))) * (HD**-0.5)
        top = jnp.max(scores, axis=0, keepdims=True)
        raised = jnp.exp(scores - top)
        attention = raised / jnp.sum(raised, axis=0, keepdims=True)
        probs[i] = attention
        held[...] = dot(attention.astype(BF16), v[rows], ((0,), (0,))).astype(BF16)
        mine[pl.ds(i * half, half)] = held[pl.ds(aligned(z0, half), half)]
        others[pl.ds(i * half, half)] = held[pl.ds(aligned(1 - z0, half), half)]


def forward(q, k, v):
    images = q.shape[0] // PATCH
    half = jax.ShapeDtypeStruct((q.shape[0] // 2, HD), BF16)
    return pl.pallas_call(
        forward_kernel,
        out_shape=[jax.ShapeDtypeStruct((images, PATCH, PATCH), F32), half, half],
        in_specs=[VMEM] * 3,
        out_specs=[VMEM] * 3,
        scratch_shapes=[pltpu.VMEM((PATCH, HD), BF16)],
        cost_estimate=COST,
        name="forward",
    )(q, k, v)


def backward_kernel(q, k, v, probs, own, from_x, from_z, from_xz, gq, gk, gv, held):
    z0 = place()["z0"]
    half = PATCH // 2
    mine = (own[...] + from_x[...].astype(F32)).astype(BF16)
    others = (from_z[...].astype(F32) + from_xz[...].astype(F32)).astype(BF16)
    for i in range(q.shape[0] // PATCH):
        held[i, pl.ds(aligned(z0, half), half)] = mine[i * half : (i + 1) * half]
        held[i, pl.ds(aligned(1 - z0, half), half)] = others[i * half : (i + 1) * half]
    for i in range(q.shape[0] // PATCH):
        rows = pl.ds(i * PATCH, PATCH)
        attention, d_att = probs[i], held[i]
        dprob = dot(v[rows], d_att, ((1,), (1,)))
        delta = jnp.sum(attention * dprob, axis=0, keepdims=True)
        dscore = (attention * (dprob - delta) * (HD**-0.5)).astype(BF16)
        gv[rows] = dot(attention.astype(BF16), d_att, ((1,), (0,))).astype(BF16)
        gk[rows] = dot(dscore, q[rows], ((1,), (0,))).astype(BF16)
        gq[rows] = dot(dscore, k[rows], ((0,), (0,))).astype(BF16)


def backward(q, k, v, probs, own, from_x, from_z, from_xz):
    images = q.shape[0] // PATCH
    return pl.pallas_call(
        backward_kernel,
        out_shape=[jax.ShapeDtypeStruct(q.shape, BF16)] * 3,
        in_specs=[VMEM] * 8,
        out_specs=[VMEM] * 3,
        scratch_shapes=[pltpu.VMEM((images, PATCH, HD), BF16)],
        cost_estimate=COST,
        name="backward",
    )(q, k, v, probs, own, from_x, from_z, from_xz)


def products_kernel(low, high, first, last, pieces, *refs):
    refs = list(refs)
    cots = [refs.pop(0) for _ in range(1 + max(ref for ref, _ in pieces))]
    w_own, w_core = refs.pop(0), refs.pop(0)
    att_own, att_x = refs.pop(0), refs.pop(0)
    before = None if first else refs.pop(0)
    keep, give = refs.pop(0), refs.pop(0)
    d_refs = refs
    at = place()
    width = high - low
    tile = min(width, 512)
    rows = []
    for n in range(4):
        z1 = 1 - at["z1"] if n // 2 else at["z1"]
        y = 1 - at["y"] if n % 2 else at["y"]
        rows.append(pl.multiple_of(z1 * 128 + y * 64, 64))
    attended = jnp.concatenate(
        [
            jnp.concatenate([att[pl.ds(row, 64)], att[pl.ds(256 + row, 64)]], axis=1)
            for att in (att_own, att_x)
            for row in rows
        ],
        axis=0,
    )
    turned = attended.T
    d = None if first else before[...]
    for other in (1, 0):
        c = 1 - at["c"] if other else at["c"]
        w_ref = w_core if other else w_own
        for start in range(0, width, tile):
            columns = pl.ds(pl.multiple_of(c * width + start, 128), tile)
            cot = jnp.concatenate(
                [cots[ref][row : row + 64, columns] for ref, row in pieces], axis=0
            )
            share = dot(turned, cot, ((1,), (0,)))
            if other:
                give[:, start : start + tile] = share.astype(BF16)
            else:
                keep[:, start : start + tile] = share
            part = dot(cot, w_ref[:, low + start : low + start + tile], ((1,), (1,)))
            d = part if d is None else d + part
    if not last:
        d_refs[0][...] = d
    else:
        for n, row in enumerate(rows):
            for g in range(2):
                share = d[(4 * g + n) * 64 : (4 * g + n + 1) * 64]
                d_refs[g][pl.ds(row, 64)] = share[:, :HD].astype(d_refs[g].dtype)
                d_refs[2 + g][pl.ds(row, 64)] = share[:, HD:].astype(BF16)


def products(low, high, pieces, cots, w_all, att, before, last):
    width = high - low
    first = before is None
    out = [
        jax.ShapeDtypeStruct((2 * HD, width), F32),
        jax.ShapeDtypeStruct((2 * HD, width), BF16),
    ]
    if last:
        out.append(jax.ShapeDtypeStruct((256, HD), F32))
        out += [jax.ShapeDtypeStruct((256, HD), BF16)] * 3
    else:
        out.append(jax.ShapeDtypeStruct((512, 2 * HD), F32))
    extra = [] if first else [before]
    return pl.pallas_call(
        functools.partial(products_kernel, low, high, first, last, pieces),
        out_shape=out,
        in_specs=[VMEM] * (len(cots) + 4 + len(extra)),
        out_specs=[VMEM] * len(out),
        cost_estimate=COST,
        name="products",
    )(*cots, *w_all, *att, *extra)


def after(value, *others):
    return lax.optimization_barrier((value, *others))[0]


CUTS = ((0, 512), (512, 1024), (1024, 1536))


def on_device_4x8(queries, keys, values, w_out, cotangent):
    m1, o1, m2, o2, m3, o3 = pack(cotangent, CUTS)
    two = lambda a, b: jnp.concatenate([a, b])
    r0 = x1, za1, ya = send(o1, x=1), send(m1, z1=1), send(two(m1, m2), y=1)
    x2, zb1, yb = send(o2, x=1), send(x1, z1=1), send(two(m3, x1), y=1)
    r1 = x2, zb1, yb
    w_z = send(after(w_out, *r0), z0=1)
    x3, za2 = send(after(o3, *r0), x=1), send(after(m2, *r0), z1=1)
    yc = send(after(two(x2, za1), *r0), y=1)
    r2 = x3, za2, yc
    zb2, yd = send(after(x2, *r1), z1=1), send(after(two(x3, zb1), *r1), y=1)
    q, k, v, *_ = lax.optimization_barrier((queries, keys, values, *r0))
    probs, mine, others = forward(q, k, v)
    att_z = send(after(others, *r1), z0=1)
    r3 = zb2, yd, w_z, att_z
    za3, ye = send(after(m3, *r2), z1=1), send(after(two(za2, zb2), *r2), y=1)
    w_own = two(w_out, w_z)
    w_c = send(after(w_own, *r2), c=1)
    att = two(mine, att_z)
    att_x = send(after(att, *r2), x=1)
    r4 = za3, ye, w_c, att_x
    zb3, yf = send(after(x3, *r3), z1=1), send(after(za3, *r3), y=1)
    r5 = zb3, yf
    yg = send(after(zb3, *r4), y=1)
    w_all, att = [w_own, w_c], [att, att_x]
    inputs = [
        ([m1, ya, za1, yc, x1, yb, zb1, yd], [0, 0, 0, 64, 0, 64, 0, 64]),
        ([m2, ya, za2, ye, x2, yc, zb2, ye], [0, 64, 0, 0, 0, 0, 0, 64]),
        ([m3, yb, za3, yf, x3, yd, zb3, yg], [0, 0, 0, 0, 0, 0, 0, 0]),
    ]
    before, parts, pairs = None, [], []
    for n, (low, high) in enumerate(CUTS):
        last = n == len(CUTS) - 1
        cots, rows = inputs[n]
        pieces = list(enumerate(rows))
        keep, give, *d = products(low, high, pieces, cots, w_all, att, before, last)
        total = keep + send(give, c=1).astype(F32)
        to_pair = total[HD:].astype(BF16)
        pair = send(to_pair, z0=1)
        before = after(d[0], to_pair, *pairs) if n == len(CUTS) - 2 else d[0]
        pairs.append(pair)
        parts.append((total[:HD] + pair.astype(F32)).astype(BF16))
    own, to_x, to_z, to_xz = d
    grad_q, grad_k, grad_v = backward(
        q, k, v, probs, own, send(to_x, x=1), send(to_z, z0=1), send(to_xz, x=1, z0=1)
    )
    return grad_q, grad_k, grad_v, jnp.concatenate(parts, axis=1)


def solution(mesh):
    in_specs = (P("dp", "mp"), P("dp", "mp"), P("dp", "mp"), P("mp", "dp"), P(("dp", "mp"), None))
    out_specs = (P("dp", "mp"), P("dp", "mp"), P("dp", "mp"), P("mp", "dp"))
    small = mesh.shape["dp"] == 4 and mesh.shape["mp"] == 8
    return jax.shard_map(
        on_device_4x8 if small else on_device,
        mesh=mesh,
        in_specs=in_specs,
        out_specs=out_specs,
        check_vma=False,
    )
```

```python
import functools

import jax
import jax.numpy as jnp
from jax import lax
from jax.experimental import pallas as pl
from jax.experimental.pallas import tpu as pltpu
from jax.sharding import PartitionSpec as P

HD = 128
PATCH = 256
AXES = ("dp", "mp")
ANY = pl.BlockSpec(memory_space=pl.ANY)
VMEM = pl.BlockSpec(memory_space=pltpu.VMEM)
F32 = jnp.float32
COST = pl.CostEstimate(flops=2 * 10**10, bytes_accessed=1 << 20, transcendentals=0)
BF16 = jnp.bfloat16


def forward_attention(queries, keys, values):
    images = queries.shape[0] // PATCH
    heads_here = queries.shape[1] // HD
    shape_four = (images, PATCH, heads_here, HD)
    scale = HD ** (-0.5)
    query_four = queries.reshape(shape_four)
    key_four = keys.reshape(shape_four)
    value_four = values.reshape(shape_four)
    scores = (
        jnp.einsum("iqhd,ikhd->ihqk", query_four, key_four, preferred_element_type=jnp.float32)
        * scale
    )
    attention = jax.nn.softmax(scores, axis=-1)
    rounded = attention.astype(jnp.bfloat16)
    attended = jnp.einsum(
        "ihqk,ikhd->iqhd", rounded, value_four, preferred_element_type=jnp.float32
    ).astype(jnp.bfloat16)
    return (attended.reshape(queries.shape), attention, rounded)


def backward_attention(queries, keys, values, d_att, attention, rounded):
    images = queries.shape[0] // PATCH
    heads_here = queries.shape[1] // HD
    shape_four = (images, PATCH, heads_here, HD)
    scale = HD ** (-0.5)
    query_four = queries.reshape(shape_four)
    key_four = keys.reshape(shape_four)
    value_four = values.reshape(shape_four)
    grad_four = d_att.reshape(shape_four)
    dprob = jnp.einsum("iqhd,ikhd->ihqk", grad_four, value_four, preferred_element_type=jnp.float32)
    delta = jnp.sum(attention * dprob, axis=-1, keepdims=True)
    dscore = (attention * (dprob - delta) * scale).astype(jnp.bfloat16)
    grad_q = jnp.einsum(
        "ihqk,ikhd->iqhd", dscore, key_four, preferred_element_type=jnp.float32
    ).astype(jnp.bfloat16)
    grad_k = jnp.einsum(
        "ihqk,iqhd->ikhd", dscore, query_four, preferred_element_type=jnp.float32
    ).astype(jnp.bfloat16)
    grad_v = jnp.einsum(
        "ihqk,iqhd->ikhd", rounded, grad_four, preferred_element_type=jnp.float32
    ).astype(jnp.bfloat16)
    return (
        grad_q.reshape(queries.shape),
        grad_k.reshape(queries.shape),
        grad_v.reshape(queries.shape),
    )


def on_device(queries, keys, values, w_out, cotangent):
    attended, attention, rounded = forward_attention(queries, keys, values)
    cot_full = lax.all_gather(cotangent, "mp", axis=0, tiled=True)
    d_full = lax.dot_general(
        cot_full,
        lax.all_gather(w_out, "dp", axis=1, tiled=True),
        (((1,), (1,)), ((), ())),
        preferred_element_type=jnp.float32,
    )
    grad_part = lax.dot_general(
        attended, cot_full, (((0,), (0,)), ((), ())), preferred_element_type=jnp.float32
    )
    d_att = d_full.astype(jnp.bfloat16)
    grad_q, grad_k, grad_v = backward_attention(queries, keys, values, d_att, attention, rounded)
    grad_weight = lax.psum_scatter(
        grad_part.astype(jnp.bfloat16), "dp", scatter_dimension=1, tiled=True
    )
    return (grad_q, grad_k, grad_v, grad_weight)


def flip(x=0, c=0, z1=0, z0=0, y=0):
    mask = (x * 2 + c) * 8 + z1 * 4 + z0 * 2 + y
    return [(i, i ^ mask) for i in range(32)]


def send(value, **bits):
    return lax.ppermute(value, AXES, flip(**bits))


def place():
    dp, mp = lax.axis_index("dp"), lax.axis_index("mp")
    return {"x": dp // 2, "c": dp % 2, "z1": mp // 4, "z0": (mp // 2) % 2, "y": mp % 2}


def aligned(index, unit):
    return pl.multiple_of(index * unit, unit)


def pack_kernel(cuts, cot, *outs):
    x = place()["x"]
    quarter = cot.shape[1] // 4
    for n, (low, high) in enumerate(cuts):
        width = high - low
        for other in range(2):
            half = 1 - x if other else x
            for c in range(2):
                start = pl.multiple_of(half * (2 * quarter) + (c * quarter + low), 128)
                outs[2 * n + other][:, c * width : (c + 1) * width] = cot[:, pl.ds(start, width)]


def pack(cot, cuts):
    shapes = []
    for low, high in cuts:
        shapes += [jax.ShapeDtypeStruct((cot.shape[0], 2 * (high - low)), cot.dtype)] * 2
    return pl.pallas_call(
        functools.partial(pack_kernel, cuts),
        out_shape=shapes,
        in_specs=[VMEM],
        out_specs=[VMEM] * len(shapes),
        cost_estimate=COST,
        name="pack",
    )(cot)


def dot(a, b, over):
    return lax.dot_general(a, b, ((over[0], over[1]), ((), ())), preferred_element_type=F32)


def forward_kernel(q, k, v, probs, mine, others, held):
    z0 = place()["z0"]
    half = PATCH // 2
    for i in range(q.shape[0] // PATCH):
        rows = pl.ds(i * PATCH, PATCH)
        scores = dot(k[rows], q[rows], ((1,), (1,))) * (HD**-0.5)
        top = jnp.max(scores, axis=0, keepdims=True)
        raised = jnp.exp(scores - top)
        attention = raised / jnp.sum(raised, axis=0, keepdims=True)
        probs[i] = attention
        held[...] = dot(attention.astype(BF16), v[rows], ((0,), (0,))).astype(BF16)
        mine[pl.ds(i * half, half)] = held[pl.ds(aligned(z0, half), half)]
        others[pl.ds(i * half, half)] = held[pl.ds(aligned(1 - z0, half), half)]


def forward(q, k, v):
    images = q.shape[0] // PATCH
    half = jax.ShapeDtypeStruct((q.shape[0] // 2, HD), BF16)
    return pl.pallas_call(
        forward_kernel,
        out_shape=[jax.ShapeDtypeStruct((images, PATCH, PATCH), F32), half, half],
        in_specs=[VMEM] * 3,
        out_specs=[VMEM] * 3,
        scratch_shapes=[pltpu.VMEM((PATCH, HD), BF16)],
        cost_estimate=COST,
        name="forward",
    )(q, k, v)


def backward_kernel(q, k, v, probs, own, from_x, from_z, from_xz, gq, gk, gv, held):
    z0 = place()["z0"]
    half = PATCH // 2
    mine = (own[...] + from_x[...].astype(F32)).astype(BF16)
    others = (from_z[...].astype(F32) + from_xz[...].astype(F32)).astype(BF16)
    for i in range(q.shape[0] // PATCH):
        held[i, pl.ds(aligned(z0, half), half)] = mine[i * half : (i + 1) * half]
        held[i, pl.ds(aligned(1 - z0, half), half)] = others[i * half : (i + 1) * half]
    for i in range(q.shape[0] // PATCH):
        rows = pl.ds(i * PATCH, PATCH)
        attention, d_att = probs[i], held[i]
        dprob = dot(v[rows], d_att, ((1,), (1,)))
        delta = jnp.sum(attention * dprob, axis=0, keepdims=True)
        dscore = (attention * (dprob - delta) * (HD**-0.5)).astype(BF16)
        gv[rows] = dot(attention.astype(BF16), d_att, ((1,), (0,))).astype(BF16)
        gk[rows] = dot(dscore, q[rows], ((1,), (0,))).astype(BF16)
        gq[rows] = dot(dscore, k[rows], ((0,), (0,))).astype(BF16)


def backward(q, k, v, probs, own, from_x, from_z, from_xz):
    images = q.shape[0] // PATCH
    return pl.pallas_call(
        backward_kernel,
        out_shape=[jax.ShapeDtypeStruct(q.shape, BF16)] * 3,
        in_specs=[VMEM] * 8,
        out_specs=[VMEM] * 3,
        scratch_shapes=[pltpu.VMEM((images, PATCH, HD), BF16)],
        cost_estimate=COST,
        name="backward",
    )(q, k, v, probs, own, from_x, from_z, from_xz)


def products_kernel(low, high, first, last, *refs):
    refs = list(refs)
    blocks = [refs.pop(0) for _ in range(8)]
    w_own, w_core = refs.pop(0), refs.pop(0)
    att_own, att_x = refs.pop(0), refs.pop(0)
    before = None if first else refs.pop(0)
    keep, give = refs.pop(0), refs.pop(0)
    d_refs = refs
    at = place()
    width = high - low
    tile = min(width, 512)
    rows = []
    for n in range(4):
        z1 = 1 - at["z1"] if n // 2 else at["z1"]
        y = 1 - at["y"] if n % 2 else at["y"]
        rows.append(pl.multiple_of(z1 * 128 + y * 64, 64))
    attended = jnp.concatenate(
        [
            jnp.concatenate([att[pl.ds(row, 64)], att[pl.ds(256 + row, 64)]], axis=1)
            for att in (att_own, att_x)
            for row in rows
        ],
        axis=0,
    )
    turned = attended.T
    d = None if first else before[...]
    for other in (1, 0):
        c = 1 - at["c"] if other else at["c"]
        w_ref = w_core if other else w_own
        for start in range(0, width, tile):
            cot = jnp.concatenate(
                [
                    block[:, pl.ds(pl.multiple_of(c * half + start + skip, 128), tile)]
                    for block in blocks
                    for half in [block.shape[1] // 2]
                    for skip in [low if half > width else 0]
                ],
                axis=0,
            )
            share = dot(turned, cot, ((1,), (0,)))
            if other:
                give[:, start : start + tile] = share.astype(BF16)
            else:
                keep[:, start : start + tile] = share
            part = dot(cot, w_ref[:, low + start : low + start + tile], ((1,), (1,)))
            d = part if d is None else d + part
    if not last:
        d_refs[0][...] = d
    else:
        for n, row in enumerate(rows):
            for g in range(2):
                share = d[(4 * g + n) * 64 : (4 * g + n + 1) * 64]
                d_refs[g][pl.ds(row, 64)] = share[:, :HD].astype(d_refs[g].dtype)
                d_refs[2 + g][pl.ds(row, 64)] = share[:, HD:].astype(BF16)


def products(low, high, blocks, w_all, att, before, last):
    width = high - low
    first = before is None
    out = [
        jax.ShapeDtypeStruct((2 * HD, width), F32),
        jax.ShapeDtypeStruct((2 * HD, width), BF16),
    ]
    if last:
        out.append(jax.ShapeDtypeStruct((256, HD), F32))
        out += [jax.ShapeDtypeStruct((256, HD), BF16)] * 3
    else:
        out.append(jax.ShapeDtypeStruct((512, 2 * HD), F32))
    extra = [] if first else [before]
    return pl.pallas_call(
        functools.partial(products_kernel, low, high, first, last),
        out_shape=out,
        in_specs=[VMEM] * (len(blocks) + 4 + len(extra)),
        out_specs=[VMEM] * len(out),
        cost_estimate=COST,
        name="products",
    )(*blocks, *w_all, *att, *extra)


def cut(value, cuts):
    half = value.shape[1] // 2
    return [
        jnp.concatenate([value[:, low:high], value[:, half + low : half + high]], axis=1)
        for low, high in cuts
    ]


def after(value, *others):
    return lax.optimization_barrier((value, *others))[0]


CUTS = ((0, 1024), (1024, 1536))


def on_device_4x8(queries, keys, values, w_out, cotangent):
    m, o = pack(cotangent, ((0, 1536),))
    za, x, ya, w_z = send(m, z1=1), send(o, x=1), send(m, y=1), send(w_out, z0=1)
    x1, x2 = cut(x, CUTS)
    zb1 = send(x1, z1=1)
    yx = send(after(x, ya), y=1)
    q, k, v, _ = lax.optimization_barrier((queries, keys, values, x))
    probs, mine, others = forward(q, k, v)
    zb2 = send(after(x2, za), z1=1)
    sa = send(after(za, ya), y=1)
    att_z = send(others, z0=1)
    att = jnp.concatenate([mine, att_z])
    att_x = send(after(att, ya), x=1)
    w_own = after(jnp.concatenate([w_out, w_z]), yx)
    w_c = send(w_own, c=1)
    sb1 = send(after(zb1, yx), y=1)
    sb2 = send(after(zb2, sa), y=1)
    w_all, att = [w_own, w_c], [after(att, zb2), att_x]
    inputs = [[m, ya, za, sa, x, yx, zb1, sb1], [m, ya, za, sa, x, yx, zb2, sb2]]
    before, parts, pairs = None, [], []
    for n, (low, high) in enumerate(CUTS):
        last = n == len(CUTS) - 1
        keep, give, *d = products(low, high, inputs[n], w_all, att, before, last)
        total = keep + send(give, c=1).astype(F32)
        to_pair = total[HD:].astype(BF16)
        pair = send(to_pair, z0=1)
        before = after(d[0], to_pair) if n == len(CUTS) - 2 else d[0]
        pairs.append(pair)
        parts.append((total[:HD] + pair.astype(F32)).astype(BF16))
    own, to_x, to_z, to_xz = d
    q = after(q, *pairs[:-1])
    grad_q, grad_k, grad_v = backward(
        q, k, v, probs, own, send(to_x, x=1), send(to_z, z0=1), send(to_xz, x=1, z0=1)
    )
    return grad_q, grad_k, grad_v, jnp.concatenate(parts, axis=1)


def solution(mesh):
    in_specs = (P("dp", "mp"), P("dp", "mp"), P("dp", "mp"), P("mp", "dp"), P(("dp", "mp"), None))
    out_specs = (P("dp", "mp"), P("dp", "mp"), P("dp", "mp"), P("mp", "dp"))
    small = mesh.shape["dp"] == 4 and mesh.shape["mp"] == 8
    return jax.shard_map(
        on_device_4x8 if small else on_device,
        mesh=mesh,
        in_specs=in_specs,
        out_specs=out_specs,
        check_vma=False,
    )
```

```python
import functools

import jax
import jax.numpy as jnp
from jax import lax
from jax.experimental import pallas as pl
from jax.experimental.pallas import tpu as pltpu
from jax.sharding import PartitionSpec as P

HD = 128
PATCH = 256
AXES = ("dp", "mp")
ANY = pl.BlockSpec(memory_space=pl.ANY)
VMEM = pl.BlockSpec(memory_space=pltpu.VMEM)
F32 = jnp.float32
SMALL, LARGE = 10**9, 2 * 10**10
BF16 = jnp.bfloat16


def forward_attention(queries, keys, values):
    images = queries.shape[0] // PATCH
    heads_here = queries.shape[1] // HD
    shape_four = (images, PATCH, heads_here, HD)
    scale = HD ** (-0.5)
    query_four = queries.reshape(shape_four)
    key_four = keys.reshape(shape_four)
    value_four = values.reshape(shape_four)
    scores = (
        jnp.einsum("iqhd,ikhd->ihqk", query_four, key_four, preferred_element_type=jnp.float32)
        * scale
    )
    attention = jax.nn.softmax(scores, axis=-1)
    rounded = attention.astype(jnp.bfloat16)
    attended = jnp.einsum(
        "ihqk,ikhd->iqhd", rounded, value_four, preferred_element_type=jnp.float32
    ).astype(jnp.bfloat16)
    return (attended.reshape(queries.shape), attention, rounded)


def backward_attention(queries, keys, values, d_att, attention, rounded):
    images = queries.shape[0] // PATCH
    heads_here = queries.shape[1] // HD
    shape_four = (images, PATCH, heads_here, HD)
    scale = HD ** (-0.5)
    query_four = queries.reshape(shape_four)
    key_four = keys.reshape(shape_four)
    value_four = values.reshape(shape_four)
    grad_four = d_att.reshape(shape_four)
    dprob = jnp.einsum("iqhd,ikhd->ihqk", grad_four, value_four, preferred_element_type=jnp.float32)
    delta = jnp.sum(attention * dprob, axis=-1, keepdims=True)
    dscore = (attention * (dprob - delta) * scale).astype(jnp.bfloat16)
    grad_q = jnp.einsum(
        "ihqk,ikhd->iqhd", dscore, key_four, preferred_element_type=jnp.float32
    ).astype(jnp.bfloat16)
    grad_k = jnp.einsum(
        "ihqk,iqhd->ikhd", dscore, query_four, preferred_element_type=jnp.float32
    ).astype(jnp.bfloat16)
    grad_v = jnp.einsum(
        "ihqk,iqhd->ikhd", rounded, grad_four, preferred_element_type=jnp.float32
    ).astype(jnp.bfloat16)
    return (
        grad_q.reshape(queries.shape),
        grad_k.reshape(queries.shape),
        grad_v.reshape(queries.shape),
    )


def on_device(queries, keys, values, w_out, cotangent):
    attended, attention, rounded = forward_attention(queries, keys, values)
    cot_full = lax.all_gather(cotangent, "mp", axis=0, tiled=True)
    d_full = lax.dot_general(
        cot_full,
        lax.all_gather(w_out, "dp", axis=1, tiled=True),
        (((1,), (1,)), ((), ())),
        preferred_element_type=jnp.float32,
    )
    grad_part = lax.dot_general(
        attended, cot_full, (((0,), (0,)), ((), ())), preferred_element_type=jnp.float32
    )
    d_att = d_full.astype(jnp.bfloat16)
    grad_q, grad_k, grad_v = backward_attention(queries, keys, values, d_att, attention, rounded)
    grad_weight = lax.psum_scatter(
        grad_part.astype(jnp.bfloat16), "dp", scatter_dimension=1, tiled=True
    )
    return (grad_q, grad_k, grad_v, grad_weight)


def flip(x=0, c=0, z1=0, z0=0, y=0):
    mask = (x * 2 + c) * 8 + z1 * 4 + z0 * 2 + y
    return [(i, i ^ mask) for i in range(32)]


def send(value, **bits):
    return lax.ppermute(value, AXES, flip(**bits))


def place():
    dp, mp = lax.axis_index("dp"), lax.axis_index("mp")
    return {"x": dp // 2, "c": dp % 2, "z1": mp // 4, "z0": (mp // 2) % 2, "y": mp % 2}


def aligned(index, unit):
    return pl.multiple_of(index * unit, unit)


def call(name, kernel, outs, ins, cost, scratch=()):
    return pl.pallas_call(
        kernel,
        out_shape=[jax.ShapeDtypeStruct(shape, kind) for shape, kind in outs],
        in_specs=[VMEM] * len(ins),
        out_specs=[VMEM] * len(outs),
        scratch_shapes=list(scratch),
        cost_estimate=pl.CostEstimate(flops=cost, bytes_accessed=1 << 20, transcendentals=0),
        compiler_params=pltpu.CompilerParams(vmem_limit_bytes=16 << 20),
        name=name,
    )(*(pltpu.with_memory_space_constraint(value, pltpu.VMEM) for value in ins))


def pack_kernel(cuts, cot, *outs):
    outs, token = outs[:-1], outs[-1]
    token[...] = jnp.zeros_like(token)
    x = place()["x"]
    quarter = cot.shape[1] // 4
    for n, (low, high) in enumerate(cuts):
        width = high - low
        for other in range(2):
            half = 1 - x if other else x
            for c in range(2):
                start = pl.multiple_of(half * (2 * quarter) + (c * quarter + low), 128)
                outs[2 * n + other][:, c * width : (c + 1) * width] = cot[:, pl.ds(start, width)]


def pack(cot, cuts):
    outs = []
    for low, high in cuts:
        outs += [((cot.shape[0], 2 * (high - low)), BF16)] * 2
    outs.append(((8, 128), F32))
    return call("pack", functools.partial(pack_kernel, cuts), outs, [cot], SMALL)


def dot(a, b, over):
    return lax.dot_general(a, b, ((over[0], over[1]), ((), ())), preferred_element_type=F32)


def forward_kernel(q, k, v, probs, mine, others, held):
    z0 = place()["z0"]
    half = PATCH // 2
    for i in range(q.shape[0] // PATCH):
        rows = pl.ds(i * PATCH, PATCH)
        scores = dot(k[rows], q[rows], ((1,), (1,))) * (HD**-0.5)
        top = jnp.max(scores, axis=0, keepdims=True)
        raised = jnp.exp(scores - top)
        attention = raised / jnp.sum(raised, axis=0, keepdims=True)
        probs[i] = attention
        held[...] = dot(attention.astype(BF16), v[rows], ((0,), (0,))).astype(BF16)
        mine[pl.ds(i * half, half)] = held[pl.ds(aligned(z0, half), half)]
        others[pl.ds(i * half, half)] = held[pl.ds(aligned(1 - z0, half), half)]


def forward(q, k, v):
    images = q.shape[0] // PATCH
    half = ((q.shape[0] // 2, HD), BF16)
    outs = [((images, PATCH, PATCH), F32), half, half]
    return call("forward", forward_kernel, outs, [q, k, v], SMALL, [pltpu.VMEM((PATCH, HD), BF16)])


def backward_kernel(at, q, k, v, probs, own, from_x, from_z, from_xz, gq, gk, gv, held):
    del at
    z0 = place()["z0"]
    half = PATCH // 2
    mine = (own[...] + from_x[...].astype(F32)).astype(BF16)
    others = (from_z[...].astype(F32) + from_xz[...].astype(F32)).astype(BF16)
    for i in range(q.shape[0] // PATCH):
        held[i, pl.ds(aligned(z0, half), half)] = mine[i * half : (i + 1) * half]
        held[i, pl.ds(aligned(1 - z0, half), half)] = others[i * half : (i + 1) * half]
    for i in range(q.shape[0] // PATCH):
        rows = pl.ds(i * PATCH, PATCH)
        attention, d_att = probs[i], held[i]
        dprob = dot(v[rows], d_att, ((1,), (1,)))
        delta = jnp.sum(attention * dprob, axis=0, keepdims=True)
        dscore = (attention * (dprob - delta) * (HD**-0.5)).astype(BF16)
        gv[rows] = dot(attention.astype(BF16), d_att, ((1,), (0,))).astype(BF16)
        gk[rows] = dot(dscore, q[rows], ((1,), (0,))).astype(BF16)
        gq[rows] = dot(dscore, k[rows], ((0,), (0,))).astype(BF16)


def backward(at, q, k, v, probs, own, from_x, from_z, from_xz):
    images = q.shape[0] // PATCH
    ins = [at, q, k, v, probs, own, from_x, from_z, from_xz]
    scratch = [pltpu.VMEM((images, PATCH, HD), BF16)]
    return call("backward", backward_kernel, [(q.shape, BF16)] * 3, ins, LARGE, scratch)


def products_kernel(low, high, first, last, *refs):
    refs = list(refs)
    blocks = [refs.pop(0) for _ in range(8)]
    w_refs = [refs.pop(0) for _ in range(2)]
    att = [refs.pop(0) for _ in range(2)]
    before = None if first else refs.pop(0)
    keep, give = refs.pop(0), refs.pop(0)
    d_refs = refs
    at = place()
    width = high - low
    tile = min(width, 512)
    rows = []
    for n in range(4):
        z1 = 1 - at["z1"] if n // 2 else at["z1"]
        y = 1 - at["y"] if n % 2 else at["y"]
        rows.append(pl.multiple_of(z1 * 128 + y * 64, 64))
    attended = jnp.concatenate(
        [
            jnp.concatenate([att[g][pl.ds(row, 64)], att[g][pl.ds(256 + row, 64)]], axis=1)
            for g in range(2)
            for row in rows
        ],
        axis=0,
    )
    turned = attended.T
    d = None if first else before[...]
    for other in (1, 0):
        c = 1 - at["c"] if other else at["c"]
        for start in range(0, width, tile):
            cot = jnp.concatenate(
                [
                    block[:, pl.ds(pl.multiple_of(c * half + start + skip, 128), tile)]
                    for block in blocks
                    for half in [block.shape[1] // 2]
                    for skip in [low if half > width else 0]
                ],
                axis=0,
            )
            share = dot(turned, cot, ((1,), (0,)))
            if other:
                give[:, start : start + tile] = share.astype(BF16)
            else:
                keep[:, start : start + tile] = share
            part = dot(cot, w_refs[other][:, low + start : low + start + tile], ((1,), (1,)))
            d = part if d is None else d + part
    if not last:
        d_refs[0][...] = d
    else:
        for n, row in enumerate(rows):
            for g in range(2):
                share = d[(4 * g + n) * 64 : (4 * g + n + 1) * 64]
                d_refs[g][pl.ds(row, 64)] = share[:, :HD].astype(d_refs[g].dtype)
                d_refs[2 + g][pl.ds(row, 64)] = share[:, HD:].astype(BF16)


def products(low, high, blocks, w_all, att, before, last):
    width = high - low
    outs = [((2 * HD, width), F32), ((2 * HD, width), BF16)]
    if last:
        outs += [((256, HD), F32)] + [((256, HD), BF16)] * 3
    else:
        outs += [((512, 2 * HD), F32)]
    first = before is None
    ins = [*blocks, *w_all, *att] + ([] if first else [before])
    kernel = functools.partial(products_kernel, low, high, first, last)
    return call("products", kernel, outs, ins, LARGE)


def fence_kernel(token, out):
    out[...] = token[...]


def fence(token, *others):
    token = after(token, *others)
    return call("fence", fence_kernel, [(token.shape, token.dtype)], [token], LARGE)[0]


def after(value, *others):
    return lax.optimization_barrier((value, *others))[0]


def two(a, b):
    return jnp.concatenate([a, b])


def cut(value, cuts):
    half = value.shape[1] // 2
    return [
        jnp.concatenate([value[:, low:high], value[:, half + low : half + high]], axis=1)
        for low, high in cuts
    ]


def after(value, *others):
    return lax.optimization_barrier((value, *others))[0]


CUTS = ((0, 1024), (1024, 1536))


def on_device_4x8(queries, keys, values, w_out, cotangent):
    m, o, at = pack(cotangent, ((0, 1536),))
    za, x, ya = send(m, z1=1), send(o, x=1), send(m, y=1)
    at = fence(at)
    q, k, v, _ = lax.optimization_barrier((queries, keys, values, at))
    probs, mine, others = forward(q, k, v)
    att_z = send(others, z0=1)
    x1, x2 = cut(x, CUTS)
    zb1 = send(x1, z1=1)
    at = fence(at, x, mine)
    yx = send(after(x, ya, at), y=1)
    att = two(mine, att_z)
    att_x = send(after(att, at), x=1)
    at = fence(at, ya, att_z)
    w_z = send(after(w_out, at), z0=1)
    zb2 = send(after(x2, za, at), z1=1)
    sa = send(after(za, at), y=1)
    at = fence(at, za, att_x)
    w_own = after(two(w_out, w_z), at)
    w_c = send(w_own, c=1)
    at = fence(at, yx, w_z)
    sb1 = send(after(zb1, at), y=1)
    at = fence(at, zb1, w_c)
    sb2 = send(after(zb2, at), y=1)
    at = fence(at, zb2)
    w_all, att = [w_own, w_c], [att, att_x]
    inputs = [[m, ya, za, sa, x, yx, zb1, sb1], [m, ya, za, sa, x, yx, zb2, sb2]]
    before, parts, pairs = None, [], []
    for n, (low, high) in enumerate(CUTS):
        last = n == len(CUTS) - 1
        att[0] = after(att[0], at)
        keep, give, *d = products(low, high, inputs[n], w_all, att, before, last)
        before = d[0]
        total = keep + send(give, c=1).astype(F32)
        to_pair = total[HD:].astype(BF16)
        pair = send(to_pair, z0=1)
        at = fence(at, to_pair)
        parts.append((total[:HD] + pair.astype(F32)).astype(BF16))
    own, to_x, to_z, to_xz = d
    grad_q, grad_k, grad_v = backward(
        at, q, k, v, probs, own, send(to_x, x=1), send(to_z, z0=1), send(to_xz, x=1, z0=1)
    )
    return grad_q, grad_k, grad_v, jnp.concatenate(parts, axis=1)


def solution(mesh):
    in_specs = (P("dp", "mp"), P("dp", "mp"), P("dp", "mp"), P("mp", "dp"), P(("dp", "mp"), None))
    out_specs = (P("dp", "mp"), P("dp", "mp"), P("dp", "mp"), P("mp", "dp"))
    small = mesh.shape["dp"] == 4 and mesh.shape["mp"] == 8
    return jax.shard_map(
        on_device_4x8 if small else on_device,
        mesh=mesh,
        in_specs=in_specs,
        out_specs=out_specs,
        check_vma=False,
    )
```

```python
import functools

import jax
import jax.numpy as jnp
from jax import lax
from jax.experimental import pallas as pl
from jax.experimental.pallas import tpu as pltpu
from jax.sharding import PartitionSpec as P

HD = 128
PATCH = 256
AXES = ("dp", "mp")
ANY = pl.BlockSpec(memory_space=pl.ANY)
VMEM = pl.BlockSpec(memory_space=pltpu.VMEM)
F32 = jnp.float32
SMALL, LARGE = 1, 10000000000
BF16 = jnp.bfloat16


def forward_attention(queries, keys, values):
    images = queries.shape[0] // PATCH
    heads_here = queries.shape[1] // HD
    shape_four = (images, PATCH, heads_here, HD)
    scale = HD ** (-0.5)
    query_four = queries.reshape(shape_four)
    key_four = keys.reshape(shape_four)
    value_four = values.reshape(shape_four)
    scores = (
        jnp.einsum("iqhd,ikhd->ihqk", query_four, key_four, preferred_element_type=jnp.float32)
        * scale
    )
    attention = jax.nn.softmax(scores, axis=-1)
    rounded = attention.astype(jnp.bfloat16)
    attended = jnp.einsum(
        "ihqk,ikhd->iqhd", rounded, value_four, preferred_element_type=jnp.float32
    ).astype(jnp.bfloat16)
    return (attended.reshape(queries.shape), attention, rounded)


def backward_attention(queries, keys, values, d_att, attention, rounded):
    images = queries.shape[0] // PATCH
    heads_here = queries.shape[1] // HD
    shape_four = (images, PATCH, heads_here, HD)
    scale = HD ** (-0.5)
    query_four = queries.reshape(shape_four)
    key_four = keys.reshape(shape_four)
    value_four = values.reshape(shape_four)
    grad_four = d_att.reshape(shape_four)
    dprob = jnp.einsum("iqhd,ikhd->ihqk", grad_four, value_four, preferred_element_type=jnp.float32)
    delta = jnp.sum(attention * dprob, axis=-1, keepdims=True)
    dscore = (attention * (dprob - delta) * scale).astype(jnp.bfloat16)
    grad_q = jnp.einsum(
        "ihqk,ikhd->iqhd", dscore, key_four, preferred_element_type=jnp.float32
    ).astype(jnp.bfloat16)
    grad_k = jnp.einsum(
        "ihqk,iqhd->ikhd", dscore, query_four, preferred_element_type=jnp.float32
    ).astype(jnp.bfloat16)
    grad_v = jnp.einsum(
        "ihqk,iqhd->ikhd", rounded, grad_four, preferred_element_type=jnp.float32
    ).astype(jnp.bfloat16)
    return (
        grad_q.reshape(queries.shape),
        grad_k.reshape(queries.shape),
        grad_v.reshape(queries.shape),
    )


def on_device(queries, keys, values, w_out, cotangent):
    attended, attention, rounded = forward_attention(queries, keys, values)
    cot_full = lax.all_gather(cotangent, "mp", axis=0, tiled=True)
    d_full = lax.dot_general(
        cot_full,
        lax.all_gather(w_out, "dp", axis=1, tiled=True),
        (((1,), (1,)), ((), ())),
        preferred_element_type=jnp.float32,
    )
    grad_part = lax.dot_general(
        attended, cot_full, (((0,), (0,)), ((), ())), preferred_element_type=jnp.float32
    )
    d_att = d_full.astype(jnp.bfloat16)
    grad_q, grad_k, grad_v = backward_attention(queries, keys, values, d_att, attention, rounded)
    grad_weight = lax.psum_scatter(
        grad_part.astype(jnp.bfloat16), "dp", scatter_dimension=1, tiled=True
    )
    return (grad_q, grad_k, grad_v, grad_weight)


def flip(x=0, c=0, z1=0, z0=0, y=0):
    mask = (x * 2 + c) * 8 + z1 * 4 + z0 * 2 + y
    return [(i, i ^ mask) for i in range(32)]


def send(value, **bits):
    return lax.ppermute(value, AXES, flip(**bits))


def place():
    dp, mp = lax.axis_index("dp"), lax.axis_index("mp")
    return {"x": dp // 2, "c": dp % 2, "z1": mp // 4, "z0": (mp // 2) % 2, "y": mp % 2}


def aligned(index, unit):
    return pl.multiple_of(index * unit, unit)


def call(name, kernel, outs, ins, cost, scratch=()):
    return pl.pallas_call(
        kernel,
        out_shape=[jax.ShapeDtypeStruct(shape, kind) for shape, kind in outs],
        in_specs=[VMEM] * len(ins),
        out_specs=[VMEM] * len(outs),
        scratch_shapes=list(scratch),
        cost_estimate=pl.CostEstimate(flops=cost, bytes_accessed=1 << 20, transcendentals=0),
        compiler_params=pltpu.CompilerParams(vmem_limit_bytes=16 << 20),
        name=name,
    )(*(pltpu.with_memory_space_constraint(value, pltpu.VMEM) for value in ins))


def pack_kernel(cuts, cot, *outs):
    outs, token = outs[:-1], outs[-1]
    token[...] = jnp.zeros_like(token)
    x = place()["x"]
    quarter = cot.shape[1] // 4
    for n, (low, high) in enumerate(cuts):
        width = high - low
        for other in range(2):
            half = 1 - x if other else x
            for c in range(2):
                start = pl.multiple_of(half * (2 * quarter) + (c * quarter + low), 128)
                outs[2 * n + other][:, c * width : (c + 1) * width] = cot[:, pl.ds(start, width)]


def pack(cot, cuts):
    outs = []
    for low, high in cuts:
        outs += [((cot.shape[0], 2 * (high - low)), BF16)] * 2
    outs.append(((8, 128), F32))
    return call("pack", functools.partial(pack_kernel, cuts), outs, [cot], SMALL)


def dot(a, b, over):
    return lax.dot_general(a, b, ((over[0], over[1]), ((), ())), preferred_element_type=F32)


def forward_kernel(q, k, v, probs, mine, others, held):
    z0 = place()["z0"]
    half = PATCH // 2
    for i in range(q.shape[0] // PATCH):
        rows = pl.ds(i * PATCH, PATCH)
        scores = dot(k[rows], q[rows], ((1,), (1,))) * (HD**-0.5)
        top = jnp.max(scores, axis=0, keepdims=True)
        raised = jnp.exp(scores - top)
        attention = raised / jnp.sum(raised, axis=0, keepdims=True)
        probs[i] = attention
        held[...] = dot(attention.astype(BF16), v[rows], ((0,), (0,))).astype(BF16)
        mine[pl.ds(i * half, half)] = held[pl.ds(aligned(z0, half), half)]
        others[pl.ds(i * half, half)] = held[pl.ds(aligned(1 - z0, half), half)]


def forward(q, k, v):
    images = q.shape[0] // PATCH
    half = ((q.shape[0] // 2, HD), BF16)
    outs = [((images, PATCH, PATCH), F32), half, half]
    return call("forward", forward_kernel, outs, [q, k, v], SMALL, [pltpu.VMEM((PATCH, HD), BF16)])


def backward_kernel(at, q, k, v, probs, own, from_x, from_z, from_xz, gq, gk, gv, held):
    del at
    z0 = place()["z0"]
    half = PATCH // 2
    mine = (own[...] + from_x[...].astype(F32)).astype(BF16)
    others = (from_z[...].astype(F32) + from_xz[...].astype(F32)).astype(BF16)
    for i in range(q.shape[0] // PATCH):
        held[i, pl.ds(aligned(z0, half), half)] = mine[i * half : (i + 1) * half]
        held[i, pl.ds(aligned(1 - z0, half), half)] = others[i * half : (i + 1) * half]
    for i in range(q.shape[0] // PATCH):
        rows = pl.ds(i * PATCH, PATCH)
        attention, d_att = probs[i], held[i]
        dprob = dot(v[rows], d_att, ((1,), (1,)))
        delta = jnp.sum(attention * dprob, axis=0, keepdims=True)
        dscore = (attention * (dprob - delta) * (HD**-0.5)).astype(BF16)
        gv[rows] = dot(attention.astype(BF16), d_att, ((1,), (0,))).astype(BF16)
        gk[rows] = dot(dscore, q[rows], ((1,), (0,))).astype(BF16)
        gq[rows] = dot(dscore, k[rows], ((0,), (0,))).astype(BF16)


def backward(at, q, k, v, probs, own, from_x, from_z, from_xz):
    images = q.shape[0] // PATCH
    ins = [at, q, k, v, probs, own, from_x, from_z, from_xz]
    scratch = [pltpu.VMEM((images, PATCH, HD), BF16)]
    return call("backward", backward_kernel, [(q.shape, BF16)] * 3, ins, LARGE, scratch)


def products_kernel(low, high, first, last, places, *refs):
    refs = list(refs[1:])
    arrays = [refs.pop(0) for _ in range(1 + max(array for array, _ in places))]
    blocks = [(arrays[array], row) for array, row in places]
    w_refs = [refs.pop(0) for _ in range(2)]
    att = [refs.pop(0) for _ in range(2)]
    before = None if first else refs.pop(0)
    keep, give = refs.pop(0), refs.pop(0)
    d_refs = refs
    at = place()
    width = high - low
    tile = next(size for size in (512, 384, 256, 128) if width % size == 0)
    rows = []
    for n in range(4):
        z1 = 1 - at["z1"] if n // 2 else at["z1"]
        y = 1 - at["y"] if n % 2 else at["y"]
        rows.append(pl.multiple_of(z1 * 128 + y * 64, 64))
    attended = jnp.concatenate(
        [
            jnp.concatenate([att[g][pl.ds(row, 64)], att[g][pl.ds(256 + row, 64)]], axis=1)
            for g in range(2)
            for row in rows
        ],
        axis=0,
    )
    turned = attended.T
    d = None if first else before[...]
    for other in (1, 0):
        c = 1 - at["c"] if other else at["c"]
        for start in range(0, width, tile):
            cot = jnp.concatenate(
                [
                    block[row : row + 64, pl.ds(pl.multiple_of(c * half + start + skip, 128), tile)]
                    for block, row in blocks
                    for half in [block.shape[1] // 2]
                    for skip in [low if half > width else 0]
                ],
                axis=0,
            )
            share = dot(turned, cot, ((1,), (0,)))
            if other:
                give[:, start : start + tile] = share.astype(BF16)
            else:
                keep[:, start : start + tile] = share
            part = dot(cot, w_refs[other][:, low + start : low + start + tile], ((1,), (1,)))
            d = part if d is None else d + part
    if not last:
        d_refs[0][...] = d
    else:
        for n, row in enumerate(rows):
            for g in range(2):
                share = d[(4 * g + n) * 64 : (4 * g + n + 1) * 64]
                d_refs[g][pl.ds(row, 64)] = share[:, :HD].astype(d_refs[g].dtype)
                d_refs[2 + g][pl.ds(row, 64)] = share[:, HD:].astype(BF16)


def products(limits, blocks, w_all, att, token, before, last):
    low, high = limits
    width = high - low
    outs = [((2 * HD, width), F32), ((2 * HD, width), BF16)]
    if last:
        outs += [((256, HD), F32)] + [((256, HD), BF16)] * 3
    else:
        outs += [((512, 2 * HD), F32)]
    arrays, places = [], []
    for array, row in blocks:
        known = [n for n, other in enumerate(arrays) if other is array]
        places.append((known[0] if known else len(arrays), row))
        if not known:
            arrays.append(array)
    ins = [token, *arrays, *w_all, *att] + ([] if before is None else [before])
    kernel = functools.partial(products_kernel, low, high, before is None, last, places)
    return call("products", kernel, outs, ins, LARGE)


def fence_kernel(token, out):
    out[...] = token[...]


def fence(token, *others, cost):
    token = after(token, *others)
    return call("fence", fence_kernel, [(token.shape, token.dtype)], [token], cost)[0]


def after(value, *others):
    return lax.optimization_barrier((value, *others))[0]


def two(a, b):
    return jnp.concatenate([a, b])


def cut(value, cuts):
    half = value.shape[1] // 2
    return [
        jnp.concatenate([value[:, low:high], value[:, half + low : half + high]], axis=1)
        for low, high in cuts
    ]


def after(value, *others):
    return lax.optimization_barrier((value, *others))[0]


CUTS = ((0, 896), (896, 1536))


def on_device_4x8(queries, keys, values, w_out, cotangent):
    m, o, m1, _, m2, _, token = pack(cotangent, ((0, CUTS[-1][1]), *CUTS))
    at0 = fence(token, cost=1)
    at1 = fence(at0, cost=10**10)
    x = send(o, x=1)
    at2 = fence(at1, x, cost=10**10)
    za = send(m, z1=1)
    probs, mine, others = forward(queries, keys, values)
    ya = send(m, y=1)
    att_z = send(after(others, at0, ya), z0=1)
    att = two(mine, att_z)
    att_x = send(att, x=1)
    at3 = fence(at2, za, att_x, cost=10**10)
    at4 = fence(at3, cost=10**10)
    x1, x2 = cut(x, CUTS)
    zb2 = send(after(x2, at3), z1=1)
    at5 = fence(at4, zb2, cost=10**10)
    att_all = [att, att_x]
    own_x = att_all[0]
    sa = send(za, y=1)
    yx = send(after(x, at2), y=1)
    zb1 = send(x1, z1=1)
    sb1 = send(zb1, y=1)
    w_z = send(after(w_out, x), z0=1)
    w_own = two(w_out, w_z)
    w_c = send(two(w_out, w_z), c=1)
    w_all = [w_own, w_c]
    blocks = [(m, 0), (ya, 0), (za, 0), (sa, 0), (x, 0), (yx, 0), (zb1, 0), (sb1, 0)]
    keep1, give1, d = products(
        CUTS[0], blocks, w_all, [own_x, att_all[1]], token, None, False
    )
    got1 = send(give1, c=1)
    total1 = keep1 + got1.astype(F32)
    to_pair1 = total1[HD:].astype(BF16)
    own_x = after(att_all[0], at4, at2)
    sb2 = send(after(zb2, at4), y=1)
    blocks = [(m, 0), (ya, 0), (za, 0), (sa, 0), (x, 0), (yx, 0), (zb2, 0), (sb2, 0)]
    keep2, give2, own, to_x, to_z, to_xz = products(
        CUTS[1], blocks, w_all, [own_x, att_all[1]], token, d, True
    )
    got2 = send(give2, c=1)
    pair1 = send(after(to_pair1, got2), z0=1)
    queries = after(queries, pair1, at1)
    from_x = send(after(to_x, at0), x=1)
    from_z = send(to_z, z0=1)
    from_xz = send(to_xz, x=1, z0=1)
    grads = backward(at5, queries, keys, values, probs, own, from_x, from_z, from_xz)
    rest1 = total1[:HD]
    part1 = (rest1 + pair1.astype(F32)).astype(BF16)
    total2 = keep2 + got2.astype(F32)
    rest2 = total2[:HD]
    to_pair2 = total2[HD:].astype(BF16)
    pair2 = send(to_pair2, z0=1)
    part2 = (rest2 + pair2.astype(F32)).astype(BF16)
    return *grads, jnp.concatenate([part1, part2], axis=1)


def solution(mesh):
    in_specs = (P("dp", "mp"), P("dp", "mp"), P("dp", "mp"), P("mp", "dp"), P(("dp", "mp"), None))
    out_specs = (P("dp", "mp"), P("dp", "mp"), P("dp", "mp"), P("mp", "dp"))
    small = mesh.shape["dp"] == 4 and mesh.shape["mp"] == 8
    return jax.shard_map(
        on_device_4x8 if small else on_device,
        mesh=mesh,
        in_specs=in_specs,
        out_specs=out_specs,
        check_vma=False,
    )
```

```python
import functools

import jax
import jax.numpy as jnp
from jax import lax
from jax.experimental import pallas as pl
from jax.experimental.pallas import tpu as pltpu
from jax.sharding import PartitionSpec as P

HD = 128
PATCH = 256
AXES = ("dp", "mp")
ANY = pl.BlockSpec(memory_space=pl.ANY)
VMEM = pl.BlockSpec(memory_space=pltpu.VMEM)
F32 = jnp.float32
SMALL, LARGE, LAST = 50000000000, 1000000000, 1000000000
BF16 = jnp.bfloat16


def forward_attention(queries, keys, values):
    images = queries.shape[0] // PATCH
    heads_here = queries.shape[1] // HD
    shape_four = (images, PATCH, heads_here, HD)
    scale = HD ** (-0.5)
    query_four = queries.reshape(shape_four)
    key_four = keys.reshape(shape_four)
    value_four = values.reshape(shape_four)
    scores = (
        jnp.einsum("iqhd,ikhd->ihqk", query_four, key_four, preferred_element_type=jnp.float32)
        * scale
    )
    attention = jax.nn.softmax(scores, axis=-1)
    rounded = attention.astype(jnp.bfloat16)
    attended = jnp.einsum(
        "ihqk,ikhd->iqhd", rounded, value_four, preferred_element_type=jnp.float32
    ).astype(jnp.bfloat16)
    return (attended.reshape(queries.shape), attention, rounded)


def backward_attention(queries, keys, values, d_att, attention, rounded):
    images = queries.shape[0] // PATCH
    heads_here = queries.shape[1] // HD
    shape_four = (images, PATCH, heads_here, HD)
    scale = HD ** (-0.5)
    query_four = queries.reshape(shape_four)
    key_four = keys.reshape(shape_four)
    value_four = values.reshape(shape_four)
    grad_four = d_att.reshape(shape_four)
    dprob = jnp.einsum("iqhd,ikhd->ihqk", grad_four, value_four, preferred_element_type=jnp.float32)
    delta = jnp.sum(attention * dprob, axis=-1, keepdims=True)
    dscore = (attention * (dprob - delta) * scale).astype(jnp.bfloat16)
    grad_q = jnp.einsum(
        "ihqk,ikhd->iqhd", dscore, key_four, preferred_element_type=jnp.float32
    ).astype(jnp.bfloat16)
    grad_k = jnp.einsum(
        "ihqk,iqhd->ikhd", dscore, query_four, preferred_element_type=jnp.float32
    ).astype(jnp.bfloat16)
    grad_v = jnp.einsum(
        "ihqk,iqhd->ikhd", rounded, grad_four, preferred_element_type=jnp.float32
    ).astype(jnp.bfloat16)
    return (
        grad_q.reshape(queries.shape),
        grad_k.reshape(queries.shape),
        grad_v.reshape(queries.shape),
    )


def on_device(queries, keys, values, w_out, cotangent):
    attended, attention, rounded = forward_attention(queries, keys, values)
    cot_full = lax.all_gather(cotangent, "mp", axis=0, tiled=True)
    d_full = lax.dot_general(
        cot_full,
        lax.all_gather(w_out, "dp", axis=1, tiled=True),
        (((1,), (1,)), ((), ())),
        preferred_element_type=jnp.float32,
    )
    grad_part = lax.dot_general(
        attended, cot_full, (((0,), (0,)), ((), ())), preferred_element_type=jnp.float32
    )
    d_att = d_full.astype(jnp.bfloat16)
    grad_q, grad_k, grad_v = backward_attention(queries, keys, values, d_att, attention, rounded)
    grad_weight = lax.psum_scatter(
        grad_part.astype(jnp.bfloat16), "dp", scatter_dimension=1, tiled=True
    )
    return (grad_q, grad_k, grad_v, grad_weight)


def flip(x=0, c=0, z1=0, z0=0, y=0):
    mask = (x * 2 + c) * 8 + z1 * 4 + z0 * 2 + y
    return [(i, i ^ mask) for i in range(32)]


def send(value, **bits):
    return lax.ppermute(value, AXES, flip(**bits))


def place():
    dp, mp = lax.axis_index("dp"), lax.axis_index("mp")
    return {"x": dp // 2, "c": dp % 2, "z1": mp // 4, "z0": (mp // 2) % 2, "y": mp % 2}


def aligned(index, unit):
    return pl.multiple_of(index * unit, unit)


def call(name, kernel, outs, ins, cost, scratch=()):
    return pl.pallas_call(
        kernel,
        out_shape=[jax.ShapeDtypeStruct(shape, kind) for shape, kind in outs],
        in_specs=[VMEM] * len(ins),
        out_specs=[VMEM] * len(outs),
        scratch_shapes=list(scratch),
        cost_estimate=pl.CostEstimate(flops=cost, bytes_accessed=1 << 20, transcendentals=0),
        compiler_params=pltpu.CompilerParams(vmem_limit_bytes=16 << 20),
        name=name,
    )(*(pltpu.with_memory_space_constraint(value, pltpu.VMEM) for value in ins))


def pack_kernel(cuts, cot, *outs):
    outs, token = outs[:-1], outs[-1]
    token[...] = jnp.zeros_like(token)
    x = place()["x"]
    quarter = cot.shape[1] // 4
    for n, (low, high) in enumerate(cuts):
        width = high - low
        for other in range(2):
            half = 1 - x if other else x
            for c in range(2):
                start = pl.multiple_of(half * (2 * quarter) + (c * quarter + low), 128)
                outs[2 * n + other][:, c * width : (c + 1) * width] = cot[:, pl.ds(start, width)]


def pack(cot, cuts):
    outs = []
    for low, high in cuts:
        outs += [((cot.shape[0], 2 * (high - low)), BF16)] * 2
    outs.append(((8, 128), F32))
    return call("pack", functools.partial(pack_kernel, cuts), outs, [cot], SMALL)


def dot(a, b, over):
    return lax.dot_general(a, b, ((over[0], over[1]), ((), ())), preferred_element_type=F32)


def forward_kernel(q, k, v, probs, mine, others, held):
    z0 = place()["z0"]
    half = PATCH // 2
    for i in range(q.shape[0] // PATCH):
        rows = pl.ds(i * PATCH, PATCH)
        scores = dot(k[rows], q[rows], ((1,), (1,))) * (HD**-0.5)
        top = jnp.max(scores, axis=0, keepdims=True)
        raised = jnp.exp(scores - top)
        attention = raised / jnp.sum(raised, axis=0, keepdims=True)
        probs[i] = attention
        held[...] = dot(attention.astype(BF16), v[rows], ((0,), (0,))).astype(BF16)
        mine[pl.ds(i * half, half)] = held[pl.ds(aligned(z0, half), half)]
        others[pl.ds(i * half, half)] = held[pl.ds(aligned(1 - z0, half), half)]


def forward(q, k, v):
    images = q.shape[0] // PATCH
    half = ((q.shape[0] // 2, HD), BF16)
    outs = [((images, PATCH, PATCH), F32), half, half]
    return call("forward", forward_kernel, outs, [q, k, v], SMALL, [pltpu.VMEM((PATCH, HD), BF16)])


def backward_kernel(at, q, k, v, probs, own, from_x, from_z, from_xz, gq, gk, gv, held):
    del at
    z0 = place()["z0"]
    half = PATCH // 2
    mine = (own[...] + from_x[...].astype(F32)).astype(BF16)
    others = (from_z[...].astype(F32) + from_xz[...].astype(F32)).astype(BF16)
    for i in range(q.shape[0] // PATCH):
        held[i, pl.ds(aligned(z0, half), half)] = mine[i * half : (i + 1) * half]
        held[i, pl.ds(aligned(1 - z0, half), half)] = others[i * half : (i + 1) * half]
    for i in range(q.shape[0] // PATCH):
        rows = pl.ds(i * PATCH, PATCH)
        attention, d_att = probs[i], held[i]
        dprob = dot(v[rows], d_att, ((1,), (1,)))
        delta = jnp.sum(attention * dprob, axis=0, keepdims=True)
        dscore = (attention * (dprob - delta) * (HD**-0.5)).astype(BF16)
        gv[rows] = dot(attention.astype(BF16), d_att, ((1,), (0,))).astype(BF16)
        gk[rows] = dot(dscore, q[rows], ((1,), (0,))).astype(BF16)
        gq[rows] = dot(dscore, k[rows], ((0,), (0,))).astype(BF16)


def backward(at, q, k, v, probs, own, from_x, from_z, from_xz):
    images = q.shape[0] // PATCH
    ins = [at, q, k, v, probs, own, from_x, from_z, from_xz]
    scratch = [pltpu.VMEM((images, PATCH, HD), BF16)]
    return call("backward", backward_kernel, [(q.shape, BF16)] * 3, ins, LAST, scratch)


def products_kernel(low, high, first, last, places, *refs):
    refs = list(refs[1:])
    arrays = [refs.pop(0) for _ in range(1 + max(array for array, _ in places))]
    blocks = [(arrays[array], row) for array, row in places]
    w_refs = [refs.pop(0) for _ in range(2)]
    att = [refs.pop(0) for _ in range(2)]
    before = None if first else refs.pop(0)
    keep, give = refs.pop(0), refs.pop(0)
    d_refs = refs
    at = place()
    width = high - low
    tiles = [(start, min(512, width - start)) for start in range(0, width, 512)]
    rows = []
    for n in range(4):
        z1 = 1 - at["z1"] if n // 2 else at["z1"]
        y = 1 - at["y"] if n % 2 else at["y"]
        rows.append(pl.multiple_of(z1 * 128 + y * 64, 64))
    attended = jnp.concatenate(
        [
            jnp.concatenate([att[g][pl.ds(row, 64)], att[g][pl.ds(256 + row, 64)]], axis=1)
            for g in range(2)
            for row in rows
        ],
        axis=0,
    )
    turned = attended.T
    d = None if first else before[...]
    for other in (1, 0):
        c = 1 - at["c"] if other else at["c"]
        for start, tile in tiles:
            cot = jnp.concatenate(
                [
                    block[row : row + 64, pl.ds(pl.multiple_of(c * half + start + skip, 128), tile)]
                    for block, row in blocks
                    for half in [block.shape[1] // 2]
                    for skip in [low if half > width else 0]
                ],
                axis=0,
            )
            share = dot(turned, cot, ((1,), (0,)))
            if other:
                give[:, start : start + tile] = share.astype(BF16)
            else:
                keep[:, start : start + tile] = share
            part = dot(cot, w_refs[other][:, low + start : low + start + tile], ((1,), (1,)))
            d = part if d is None else d + part
    if not last:
        d_refs[0][...] = d
    else:
        for n, row in enumerate(rows):
            for g in range(2):
                share = d[(4 * g + n) * 64 : (4 * g + n + 1) * 64]
                d_refs[g][pl.ds(row, 64)] = share[:, :HD].astype(d_refs[g].dtype)
                d_refs[2 + g][pl.ds(row, 64)] = share[:, HD:].astype(BF16)


def products(limits, blocks, w_all, att, token, before, last):
    low, high = limits
    width = high - low
    outs = [((2 * HD, width), F32), ((2 * HD, width), BF16)]
    if last:
        outs += [((256, HD), F32)] + [((256, HD), BF16)] * 3
    else:
        outs += [((512, 2 * HD), F32)]
    arrays, places = [], []
    for array, row in blocks:
        known = [n for n, other in enumerate(arrays) if other is array]
        places.append((known[0] if known else len(arrays), row))
        if not known:
            arrays.append(array)
    ins = [token, *arrays, *w_all, *att] + ([] if before is None else [before])
    kernel = functools.partial(products_kernel, low, high, before is None, last, places)
    return call("products", kernel, outs, ins, LARGE)


def fence_kernel(token, out):
    out[...] = token[...]


def fence(token, *others, cost):
    token = after(token, *others)
    return call("fence", fence_kernel, [(token.shape, token.dtype)], [token], cost)[0]


def after(value, *others):
    return lax.optimization_barrier((value, *others))[0]


def two(a, b):
    return jnp.concatenate([a, b])


def cut(value, cuts):
    half = value.shape[1] // 2
    return [
        jnp.concatenate([value[:, low:high], value[:, half + low : half + high]], axis=1)
        for low, high in cuts
    ]


def after(value, *others):
    return lax.optimization_barrier((value, *others))[0]


CUTS = ((0, 896), (896, 1536))


def on_device_4x8(queries, keys, values, w_out, cotangent):
    m, o, token = pack(cotangent, ((0, CUTS[-1][1]),))
    at0 = fence(token, cost=1)
    at1 = fence(at0, cost=10**10)
    za = send(m, z1=1)
    probs, mine, others = forward(queries, keys, values)
    ya = send(m, y=1)
    att_z = send(after(others, ya), z0=1)
    att = two(mine, att_z)
    att_x = send(after(att, ya), x=1)
    x = send(o, x=1)
    at2 = fence(at1, za, att_x, x, cost=10**10)
    at3 = fence(at2, cost=10**10)
    w_z = send(after(w_out, x, ya), z0=1)
    w_c = send(after(two(w_out, w_z), w_z), c=1)
    at4 = fence(at3, w_c, cost=2 * 10**10)
    att_all = [att, att_x]
    own_x = after(att_all[0], za)
    sa = send(after(za, att_x, ya), y=1)
    yx = send(x, y=1)
    x1, x2 = cut(x, CUTS)
    zb1 = send(x1, z1=1)
    sb1 = send(zb1, y=1)
    w_own = two(w_out, w_z)
    w_all = [w_own, w_c]
    blocks = [(m, 0), (ya, 0), (za, 0), (sa, 0), (x, 0), (yx, 0), (zb1, 0), (sb1, 0)]
    keep1, give1, d = products(
        CUTS[0], blocks, w_all, [own_x, att_all[1]], token, None, False
    )
    got1 = send(after(give1, give1, att_z), c=1)
    at5 = fence(at4, att_x, got1, cost=10**10)
    own_x = after(att_all[0], give1)
    zb2 = send(after(x2, at2, za, att_z), z1=1)
    sb2 = send(after(zb2, at3), y=1)
    blocks = [(m, 0), (ya, 0), (za, 0), (sa, 0), (x, 0), (yx, 0), (zb2, 0), (sb2, 0)]
    keep2, give2, own, to_x, to_z, to_xz = products(
        CUTS[1], blocks, w_all, [own_x, att_all[1]], token, d, True
    )
    got2 = send(give2, c=1)
    total2 = keep2 + got2.astype(F32)
    to_pair2 = total2[HD:].astype(BF16)
    pair2 = send(after(to_pair2, at2), z0=1)
    queries = after(queries, pair2, at3)
    from_x = send(after(to_x, at0, got1), x=1)
    from_z = send(after(to_z, at1), z0=1)
    from_xz = send(to_xz, x=1, z0=1)
    grads = backward(at5, queries, keys, values, probs, own, from_x, from_z, from_xz)
    total1 = keep1 + got1.astype(F32)
    rest1 = total1[:HD]
    rest2 = total2[:HD]
    rest2 = after(rest2, grads[0])
    to_pair1 = total1[HD:].astype(BF16)
    pair1 = send(after(to_pair1, at1), z0=1)
    part1 = (rest1 + pair1.astype(F32)).astype(BF16)
    part2 = (rest2 + pair2.astype(F32)).astype(BF16)
    return *grads, jnp.concatenate([part1, part2], axis=1)


def solution(mesh):
    in_specs = (P("dp", "mp"), P("dp", "mp"), P("dp", "mp"), P("mp", "dp"), P(("dp", "mp"), None))
    out_specs = (P("dp", "mp"), P("dp", "mp"), P("dp", "mp"), P("mp", "dp"))
    small = mesh.shape["dp"] == 4 and mesh.shape["mp"] == 8
    return jax.shard_map(
        on_device_4x8 if small else on_device,
        mesh=mesh,
        in_specs=in_specs,
        out_specs=out_specs,
        check_vma=False,
    )
```

```python
import functools

import jax
import jax.numpy as jnp
from jax import lax
from jax.experimental import pallas as pl
from jax.experimental.pallas import tpu as pltpu
from jax.sharding import PartitionSpec as P

HD = 128
PATCH = 256
AXES = ("dp", "mp")
ANY = pl.BlockSpec(memory_space=pl.ANY)
VMEM = pl.BlockSpec(memory_space=pltpu.VMEM)
F32 = jnp.float32
SMALL, LARGE, LAST = 1, 50000000000, 20000000000
BF16 = jnp.bfloat16


def forward_attention(queries, keys, values):
    images = queries.shape[0] // PATCH
    heads_here = queries.shape[1] // HD
    shape_four = (images, PATCH, heads_here, HD)
    scale = HD ** (-0.5)
    query_four = queries.reshape(shape_four)
    key_four = keys.reshape(shape_four)
    value_four = values.reshape(shape_four)
    scores = (
        jnp.einsum("iqhd,ikhd->ihqk", query_four, key_four, preferred_element_type=jnp.float32)
        * scale
    )
    attention = jax.nn.softmax(scores, axis=-1)
    rounded = attention.astype(jnp.bfloat16)
    attended = jnp.einsum(
        "ihqk,ikhd->iqhd", rounded, value_four, preferred_element_type=jnp.float32
    ).astype(jnp.bfloat16)
    return (attended.reshape(queries.shape), attention, rounded)


def backward_attention(queries, keys, values, d_att, attention, rounded):
    images = queries.shape[0] // PATCH
    heads_here = queries.shape[1] // HD
    shape_four = (images, PATCH, heads_here, HD)
    scale = HD ** (-0.5)
    query_four = queries.reshape(shape_four)
    key_four = keys.reshape(shape_four)
    value_four = values.reshape(shape_four)
    grad_four = d_att.reshape(shape_four)
    dprob = jnp.einsum("iqhd,ikhd->ihqk", grad_four, value_four, preferred_element_type=jnp.float32)
    delta = jnp.sum(attention * dprob, axis=-1, keepdims=True)
    dscore = (attention * (dprob - delta) * scale).astype(jnp.bfloat16)
    grad_q = jnp.einsum(
        "ihqk,ikhd->iqhd", dscore, key_four, preferred_element_type=jnp.float32
    ).astype(jnp.bfloat16)
    grad_k = jnp.einsum(
        "ihqk,iqhd->ikhd", dscore, query_four, preferred_element_type=jnp.float32
    ).astype(jnp.bfloat16)
    grad_v = jnp.einsum(
        "ihqk,iqhd->ikhd", rounded, grad_four, preferred_element_type=jnp.float32
    ).astype(jnp.bfloat16)
    return (
        grad_q.reshape(queries.shape),
        grad_k.reshape(queries.shape),
        grad_v.reshape(queries.shape),
    )


def on_device(queries, keys, values, w_out, cotangent):
    attended, attention, rounded = forward_attention(queries, keys, values)
    cot_full = lax.all_gather(cotangent, "mp", axis=0, tiled=True)
    d_full = lax.dot_general(
        cot_full,
        lax.all_gather(w_out, "dp", axis=1, tiled=True),
        (((1,), (1,)), ((), ())),
        preferred_element_type=jnp.float32,
    )
    grad_part = lax.dot_general(
        attended, cot_full, (((0,), (0,)), ((), ())), preferred_element_type=jnp.float32
    )
    d_att = d_full.astype(jnp.bfloat16)
    grad_q, grad_k, grad_v = backward_attention(queries, keys, values, d_att, attention, rounded)
    grad_weight = lax.psum_scatter(
        grad_part.astype(jnp.bfloat16), "dp", scatter_dimension=1, tiled=True
    )
    return (grad_q, grad_k, grad_v, grad_weight)


def flip(x=0, c=0, z1=0, z0=0, y=0):
    mask = (x * 2 + c) * 8 + z1 * 4 + z0 * 2 + y
    return [(i, i ^ mask) for i in range(32)]


def send(value, **bits):
    return lax.ppermute(value, AXES, flip(**bits))


def place():
    dp, mp = lax.axis_index("dp"), lax.axis_index("mp")
    return {"x": dp // 2, "c": dp % 2, "z1": mp // 4, "z0": (mp // 2) % 2, "y": mp % 2}


def aligned(index, unit):
    return pl.multiple_of(index * unit, unit)


def call(name, kernel, outs, ins, cost, scratch=()):
    return pl.pallas_call(
        kernel,
        out_shape=[jax.ShapeDtypeStruct(shape, kind) for shape, kind in outs],
        in_specs=[VMEM] * len(ins),
        out_specs=[VMEM] * len(outs),
        scratch_shapes=list(scratch),
        cost_estimate=pl.CostEstimate(flops=cost, bytes_accessed=1 << 20, transcendentals=0),
        compiler_params=pltpu.CompilerParams(vmem_limit_bytes=16 << 20),
        name=name,
    )(*(pltpu.with_memory_space_constraint(value, pltpu.VMEM) for value in ins))


def pack_kernel(cuts, cot, *outs):
    outs, token = outs[:-1], outs[-1]
    token[...] = jnp.zeros_like(token)
    x = place()["x"]
    quarter = cot.shape[1] // 4
    for n, (low, high) in enumerate(cuts):
        width = high - low
        for other in range(2):
            half = 1 - x if other else x
            for c in range(2):
                start = pl.multiple_of(half * (2 * quarter) + (c * quarter + low), 128)
                outs[2 * n + other][:, c * width : (c + 1) * width] = cot[:, pl.ds(start, width)]


def pack(cot, cuts):
    outs = []
    for low, high in cuts:
        outs += [((cot.shape[0], 2 * (high - low)), BF16)] * 2
    outs.append(((8, 128), F32))
    return call("pack", functools.partial(pack_kernel, cuts), outs, [cot], SMALL)


def dot(a, b, over):
    return lax.dot_general(a, b, ((over[0], over[1]), ((), ())), preferred_element_type=F32)


def forward_kernel(q, k, v, w, probs, mine, bundle, held):
    z0 = place()["z0"]
    bundle[:, : w.shape[1]] = w[...]
    half = PATCH // 2
    for i in range(q.shape[0] // PATCH):
        rows = pl.ds(i * PATCH, PATCH)
        scores = dot(k[rows], q[rows], ((1,), (1,))) * (HD**-0.5)
        top = jnp.max(scores, axis=0, keepdims=True)
        raised = jnp.exp(scores - top)
        attention = raised / jnp.sum(raised, axis=0, keepdims=True)
        probs[i] = attention
        held[...] = dot(attention.astype(BF16), v[rows], ((0,), (0,))).astype(BF16)
        mine[pl.ds(i * half, half)] = held[pl.ds(aligned(z0, half), half)]
        bundle[:, w.shape[1] + i * HD : w.shape[1] + (i + 1) * HD] = held[
            pl.ds(aligned(1 - z0, half), half)
        ]


def forward(q, k, v, w):
    images = q.shape[0] // PATCH
    outs = [((images, PATCH, PATCH), F32), ((q.shape[0] // 2, HD), BF16)]
    outs.append(((HD, w.shape[1] + images * HD), BF16))
    scratch = [pltpu.VMEM((PATCH, HD), BF16)]
    return call("forward", forward_kernel, outs, [q, k, v, w], SMALL, scratch)


def backward_kernel(at, q, k, v, probs, own, from_x, from_z, from_xz, gq, gk, gv, end, held):
    end[...] = at[...]
    z0 = place()["z0"]
    half = PATCH // 2
    mine = (own[...] + from_x[...].astype(F32)).astype(BF16)
    others = (from_z[...].astype(F32) + from_xz[...].astype(F32)).astype(BF16)
    for i in range(q.shape[0] // PATCH):
        held[i, pl.ds(aligned(z0, half), half)] = mine[i * half : (i + 1) * half]
        held[i, pl.ds(aligned(1 - z0, half), half)] = others[i * half : (i + 1) * half]
    for i in range(q.shape[0] // PATCH):
        rows = pl.ds(i * PATCH, PATCH)
        attention, d_att = probs[i], held[i]
        dprob = dot(v[rows], d_att, ((1,), (1,)))
        delta = jnp.sum(attention * dprob, axis=0, keepdims=True)
        dscore = (attention * (dprob - delta) * (HD**-0.5)).astype(BF16)
        gv[rows] = dot(attention.astype(BF16), d_att, ((1,), (0,))).astype(BF16)
        gk[rows] = dot(dscore, q[rows], ((1,), (0,))).astype(BF16)
        gq[rows] = dot(dscore, k[rows], ((0,), (0,))).astype(BF16)


def backward(at, q, k, v, probs, own, from_x, from_z, from_xz):
    images = q.shape[0] // PATCH
    ins = [at, q, k, v, probs, own, from_x, from_z, from_xz]
    scratch = [pltpu.VMEM((images, PATCH, HD), BF16)]
    outs = [(q.shape, BF16)] * 3 + [(at.shape, at.dtype)]
    return call("backward", backward_kernel, outs, ins, LAST, scratch)


def products_kernel(low, high, first, last, places, *refs):
    refs = list(refs[1:])
    arrays = [refs.pop(0) for _ in range(1 + max(array for array, _ in places))]
    blocks = [(arrays[array], row) for array, row in places]
    w_refs = [refs.pop(0) for _ in range(4)]
    mine, att_x = refs.pop(0), refs.pop(0)
    pairs = w_refs[1]
    before = None if first else refs.pop(0)
    keep, give = refs.pop(0), refs.pop(0)
    d_refs = refs
    at = place()
    whole = w_refs[0].shape[1]
    width = high - low
    tiles = [(start, min(512, width - start)) for start in range(0, width, 512)]
    rows, parts = [], []
    for n in range(4):
        z1 = 1 - at["z1"] if n // 2 else at["z1"]
        y = 1 - at["y"] if n % 2 else at["y"]
        rows.append(pl.multiple_of(z1 * 128 + y * 64, 64))
        spot = pl.ds(aligned(y, 64), 64), pl.ds(pl.multiple_of(whole + z1 * HD, HD), HD)
        parts.append([mine[pl.ds(rows[n], 64)], pairs[spot]])
    for row in rows:
        parts.append([att_x[pl.ds(row, 64)], att_x[pl.ds(256 + row, 64)]])
    attended = jnp.concatenate([jnp.concatenate(both, axis=1) for both in parts], axis=0)
    turned = attended.T
    d = None if first else before[...]
    for other in (1, 0):
        c = 1 - at["c"] if other else at["c"]
        for start, tile in tiles:
            cot = jnp.concatenate(
                [
                    block[row : row + 64, pl.ds(pl.multiple_of(c * half + start + skip, 128), tile)]
                    for block, row in blocks
                    for half in [block.shape[1] // 2]
                    for skip in [low if half > width else 0]
                ],
                axis=0,
            )
            share = dot(turned, cot, ((1,), (0,)))
            if other:
                give[:, start : start + tile] = share.astype(BF16)
            else:
                keep[:, start : start + tile] = share
            w = jnp.concatenate(
                [ref[:, low + start : low + start + tile] for ref in w_refs[2 * other :][:2]], axis=0
            )
            part = dot(cot, w, ((1,), (1,)))
            d = part if d is None else d + part
    if not last:
        d_refs[0][...] = d
    else:
        for n, row in enumerate(rows):
            for g in range(2):
                share = d[(4 * g + n) * 64 : (4 * g + n + 1) * 64]
                d_refs[g][pl.ds(row, 64)] = share[:, :HD].astype(d_refs[g].dtype)
                d_refs[2 + g][pl.ds(row, 64)] = share[:, HD:].astype(BF16)


def products(limits, blocks, w_all, att, token, before, last):
    low, high = limits
    width = high - low
    outs = [((2 * HD, width), F32), ((2 * HD, width), BF16)]
    if last:
        outs += [((256, HD), F32)] + [((256, HD), BF16)] * 3
    else:
        outs += [((512, 2 * HD), F32)]
    arrays, places = [], []
    for array, row in blocks:
        known = [n for n, other in enumerate(arrays) if other is array]
        places.append((known[0] if known else len(arrays), row))
        if not known:
            arrays.append(array)
    ins = [token, *arrays, *w_all, *att] + ([] if before is None else [before])
    kernel = functools.partial(products_kernel, low, high, before is None, last, places)
    return call("products", kernel, outs, ins, LARGE)


def fence_kernel(token, out):
    out[...] = token[...]


def fence(token, *others, cost):
    token = after(token, *others)
    return call("fence", fence_kernel, [(token.shape, token.dtype)], [token], cost)[0]


def finish_kernel(limits, *refs):
    out = refs[-1]
    for n, (low, high) in enumerate(limits):
        total, pair = refs[1 + 2 * n], refs[2 + 2 * n]
        out[:, low:high] = (total[:HD] + pair[...].astype(F32)).astype(BF16)


def finish(token, limits, totals, pairs):
    ins = [token, *(ref for both in zip(totals, pairs) for ref in both)]
    outs = [((HD, limits[-1][1]), BF16)]
    return call("finish", functools.partial(finish_kernel, limits), outs, ins, LAST)[0]


def after(value, *others):
    return lax.optimization_barrier((value, *others))[0]


def two(a, b):
    return jnp.concatenate([a, b])


def cut(value, cuts):
    half = value.shape[1] // 2
    return [
        jnp.concatenate([value[:, low:high], value[:, half + low : half + high]], axis=1)
        for low, high in cuts
    ]


def after(value, *others):
    return lax.optimization_barrier((value, *others))[0]


CUTS = ((0, 1024), (1024, 1536))


def on_device_4x8(queries, keys, values, w_out, cotangent):
    m, o, token = pack(cotangent, ((0, CUTS[-1][1]),))
    za = send(m, z1=1)
    ya = send(m, y=1)
    sa = send(after(za, ya), y=1)
    at0 = fence(token, sa, cost=20000000000)
    probs, mine, bundle = forward(queries, keys, values, w_out)
    pair_w = send(after(bundle, ya), z0=1)
    core_w = send(after(w_out, pair_w), c=1)
    x = send(o, x=1)
    x1, x2 = cut(x, CUTS)
    zb1 = send(x1, z1=1)
    sb1 = send(after(zb1, zb1), y=1)
    at1 = fence(at0, core_w, sb1, cost=1)
    whole = w_out.shape[1]
    att = jnp.concatenate([mine, pair_w[:, whole : whole + HD], pair_w[:, whole + HD :]])
    att_x = send(att, x=1)
    own = mine
    yx = send(x, y=1)
    core_pair_w = send(after(pair_w, za), c=1)
    w_all = [w_out, pair_w, core_w, core_pair_w]
    blocks = [(m, 0), (ya, 0), (za, 0), (sa, 0), (x, 0), (yx, 0), (zb1, 0), (sb1, 0)]
    keep1, give1, d = products(
        CUTS[0], blocks, w_all, [own, att_x], token, None, False
    )
    got1 = send(after(give1, att_x, zb1), c=1)
    total1 = keep1 + got1.astype(F32)
    to_pair1 = total1[HD:].astype(BF16)
    pair1 = send(to_pair1, z0=1)
    queries = after(queries, at1, pair1)
    own = mine
    zb2 = send(after(x2, yx), z1=1)
    sb2 = send(zb2, y=1)
    blocks = [(m, 0), (ya, 0), (za, 0), (sa, 0), (x, 0), (yx, 0), (zb2, 0), (sb2, 0)]
    keep2, give2, d, to_x, to_z, to_xz = products(
        CUTS[1], blocks, w_all, [own, att_x], token, d, True
    )
    from_x = send(after(to_x, at1), x=1)
    from_z = send(after(to_z, give1), z0=1)
    from_xz = send(to_xz, x=1, z0=1)
    *grads, end = backward(
        at1, queries, keys, values, probs, d, from_x, from_z, from_xz
    )
    got2 = send(after(give2, to_pair1), c=1)
    total2 = keep2 + got2.astype(F32)
    to_pair2 = total2[HD:].astype(BF16)
    pair2 = send(to_pair2, z0=1)
    totals, pairs = [total1, total2], [pair1, pair2]
    return *grads, finish(token, CUTS, totals, pairs)


def solution(mesh):
    in_specs = (P("dp", "mp"), P("dp", "mp"), P("dp", "mp"), P("mp", "dp"), P(("dp", "mp"), None))
    out_specs = (P("dp", "mp"), P("dp", "mp"), P("dp", "mp"), P("mp", "dp"))
    small = mesh.shape["dp"] == 4 and mesh.shape["mp"] == 8
    return jax.shard_map(
        on_device_4x8 if small else on_device,
        mesh=mesh,
        in_specs=in_specs,
        out_specs=out_specs,
        check_vma=False,
    )
```

```python
import functools

import jax
import jax.numpy as jnp
from jax import lax
from jax.experimental import pallas as pl
from jax.experimental.pallas import tpu as pltpu
from jax.sharding import PartitionSpec as P

HD = 128
PATCH = 256
AXES = ("dp", "mp")
ANY = pl.BlockSpec(memory_space=pl.ANY)
VMEM = pl.BlockSpec(memory_space=pltpu.VMEM)
F32 = jnp.float32
SMALL, LARGE, LAST = 10000000000, 10000000000, 20000000000
BF16 = jnp.bfloat16


def forward_attention(queries, keys, values):
    images = queries.shape[0] // PATCH
    heads_here = queries.shape[1] // HD
    shape_four = (images, PATCH, heads_here, HD)
    scale = HD ** (-0.5)
    query_four = queries.reshape(shape_four)
    key_four = keys.reshape(shape_four)
    value_four = values.reshape(shape_four)
    scores = (
        jnp.einsum("iqhd,ikhd->ihqk", query_four, key_four, preferred_element_type=jnp.float32)
        * scale
    )
    attention = jax.nn.softmax(scores, axis=-1)
    rounded = attention.astype(jnp.bfloat16)
    attended = jnp.einsum(
        "ihqk,ikhd->iqhd", rounded, value_four, preferred_element_type=jnp.float32
    ).astype(jnp.bfloat16)
    return (attended.reshape(queries.shape), attention, rounded)


def backward_attention(queries, keys, values, d_att, attention, rounded):
    images = queries.shape[0] // PATCH
    heads_here = queries.shape[1] // HD
    shape_four = (images, PATCH, heads_here, HD)
    scale = HD ** (-0.5)
    query_four = queries.reshape(shape_four)
    key_four = keys.reshape(shape_four)
    value_four = values.reshape(shape_four)
    grad_four = d_att.reshape(shape_four)
    dprob = jnp.einsum("iqhd,ikhd->ihqk", grad_four, value_four, preferred_element_type=jnp.float32)
    delta = jnp.sum(attention * dprob, axis=-1, keepdims=True)
    dscore = (attention * (dprob - delta) * scale).astype(jnp.bfloat16)
    grad_q = jnp.einsum(
        "ihqk,ikhd->iqhd", dscore, key_four, preferred_element_type=jnp.float32
    ).astype(jnp.bfloat16)
    grad_k = jnp.einsum(
        "ihqk,iqhd->ikhd", dscore, query_four, preferred_element_type=jnp.float32
    ).astype(jnp.bfloat16)
    grad_v = jnp.einsum(
        "ihqk,iqhd->ikhd", rounded, grad_four, preferred_element_type=jnp.float32
    ).astype(jnp.bfloat16)
    return (
        grad_q.reshape(queries.shape),
        grad_k.reshape(queries.shape),
        grad_v.reshape(queries.shape),
    )


def on_device(queries, keys, values, w_out, cotangent):
    attended, attention, rounded = forward_attention(queries, keys, values)
    cot_full = lax.all_gather(cotangent, "mp", axis=0, tiled=True)
    d_full = lax.dot_general(
        cot_full,
        lax.all_gather(w_out, "dp", axis=1, tiled=True),
        (((1,), (1,)), ((), ())),
        preferred_element_type=jnp.float32,
    )
    grad_part = lax.dot_general(
        attended, cot_full, (((0,), (0,)), ((), ())), preferred_element_type=jnp.float32
    )
    d_att = d_full.astype(jnp.bfloat16)
    grad_q, grad_k, grad_v = backward_attention(queries, keys, values, d_att, attention, rounded)
    grad_weight = lax.psum_scatter(
        grad_part.astype(jnp.bfloat16), "dp", scatter_dimension=1, tiled=True
    )
    return (grad_q, grad_k, grad_v, grad_weight)


def flip(x=0, c=0, z1=0, z0=0, y=0):
    mask = (x * 2 + c) * 8 + z1 * 4 + z0 * 2 + y
    return [(i, i ^ mask) for i in range(32)]


def send(value, **bits):
    return lax.ppermute(value, AXES, flip(**bits))


def place():
    dp, mp = lax.axis_index("dp"), lax.axis_index("mp")
    return {"x": dp // 2, "c": dp % 2, "z1": mp // 4, "z0": (mp // 2) % 2, "y": mp % 2}


def aligned(index, unit):
    return pl.multiple_of(index * unit, unit)


def call(name, kernel, outs, ins, cost, scratch=()):
    return pl.pallas_call(
        kernel,
        out_shape=[jax.ShapeDtypeStruct(shape, kind) for shape, kind in outs],
        in_specs=[VMEM] * len(ins),
        out_specs=[VMEM] * len(outs),
        scratch_shapes=list(scratch),
        cost_estimate=pl.CostEstimate(flops=cost, bytes_accessed=1 << 20, transcendentals=0),
        compiler_params=pltpu.CompilerParams(vmem_limit_bytes=16 << 20),
        name=name,
    )(*(pltpu.with_memory_space_constraint(value, pltpu.VMEM) for value in ins))


def pack_kernel(cuts, cot, *outs):
    outs, token = outs[:-1], outs[-1]
    token[...] = jnp.zeros_like(token)
    x = place()["x"]
    quarter = cot.shape[1] // 4
    for n, (low, high) in enumerate(cuts):
        width = high - low
        for other in range(2):
            half = 1 - x if other else x
            for c in range(2):
                start = pl.multiple_of(half * (2 * quarter) + (c * quarter + low), 128)
                outs[2 * n + other][:, c * width : (c + 1) * width] = cot[:, pl.ds(start, width)]


def pack(cot, cuts):
    outs = []
    for low, high in cuts:
        outs += [((cot.shape[0], 2 * (high - low)), BF16)] * 2
    outs.append(((8, 128), F32))
    return call("pack", functools.partial(pack_kernel, cuts), outs, [cot], SMALL)


def dot(a, b, over):
    return lax.dot_general(a, b, ((over[0], over[1]), ((), ())), preferred_element_type=F32)


def forward_kernel(q, k, v, w, probs, mine, bundle, held):
    z0 = place()["z0"]
    bundle[:, : w.shape[1]] = w[...]
    half = PATCH // 2
    for i in range(q.shape[0] // PATCH):
        rows = pl.ds(i * PATCH, PATCH)
        scores = dot(k[rows], q[rows], ((1,), (1,))) * (HD**-0.5)
        top = jnp.max(scores, axis=0, keepdims=True)
        raised = jnp.exp(scores - top)
        attention = raised / jnp.sum(raised, axis=0, keepdims=True)
        probs[i] = attention
        held[...] = dot(attention.astype(BF16), v[rows], ((0,), (0,))).astype(BF16)
        mine[pl.ds(i * half, half)] = held[pl.ds(aligned(z0, half), half)]
        bundle[:, w.shape[1] + i * HD : w.shape[1] + (i + 1) * HD] = held[
            pl.ds(aligned(1 - z0, half), half)
        ]


def forward(q, k, v, w):
    images = q.shape[0] // PATCH
    outs = [((images, PATCH, PATCH), F32), ((q.shape[0] // 2, HD), BF16)]
    outs.append(((HD, w.shape[1] + images * HD), BF16))
    scratch = [pltpu.VMEM((PATCH, HD), BF16)]
    return call("forward", forward_kernel, outs, [q, k, v, w], SMALL, scratch)


def backward_kernel(at, q, k, v, probs, own, from_x, from_z, from_xz, gq, gk, gv, end, held):
    end[...] = at[...]
    z0 = place()["z0"]
    half = PATCH // 2
    mine = (own[...] + from_x[...].astype(F32)).astype(BF16)
    others = (from_z[...].astype(F32) + from_xz[...].astype(F32)).astype(BF16)
    for i in range(q.shape[0] // PATCH):
        held[i, pl.ds(aligned(z0, half), half)] = mine[i * half : (i + 1) * half]
        held[i, pl.ds(aligned(1 - z0, half), half)] = others[i * half : (i + 1) * half]
    for i in range(q.shape[0] // PATCH):
        rows = pl.ds(i * PATCH, PATCH)
        attention, d_att = probs[i], held[i]
        dprob = dot(v[rows], d_att, ((1,), (1,)))
        delta = jnp.sum(attention * dprob, axis=0, keepdims=True)
        dscore = (attention * (dprob - delta) * (HD**-0.5)).astype(BF16)
        gv[rows] = dot(attention.astype(BF16), d_att, ((1,), (0,))).astype(BF16)
        gk[rows] = dot(dscore, q[rows], ((1,), (0,))).astype(BF16)
        gq[rows] = dot(dscore, k[rows], ((0,), (0,))).astype(BF16)


def backward(at, q, k, v, probs, own, from_x, from_z, from_xz):
    images = q.shape[0] // PATCH
    ins = [at, q, k, v, probs, own, from_x, from_z, from_xz]
    scratch = [pltpu.VMEM((images, PATCH, HD), BF16)]
    outs = [(q.shape, BF16)] * 3 + [(at.shape, at.dtype)]
    return call("backward", backward_kernel, outs, ins, LAST, scratch)


def products_kernel(low, high, first, last, places, *refs):
    refs = list(refs[1:])
    arrays = [refs.pop(0) for _ in range(1 + max(array for array, _ in places))]
    blocks = [(arrays[array], row) for array, row in places]
    w_refs = [refs.pop(0) for _ in range(4)]
    mine, att_x = refs.pop(0), refs.pop(0)
    pairs = w_refs[1]
    before = None if first else refs.pop(0)
    keep, give = refs.pop(0), refs.pop(0)
    d_refs = refs
    at = place()
    whole = w_refs[0].shape[1]
    width = high - low
    tiles = [(start, min(512, width - start)) for start in range(0, width, 512)]
    rows, parts = [], []
    for n in range(4):
        z1 = 1 - at["z1"] if n // 2 else at["z1"]
        y = 1 - at["y"] if n % 2 else at["y"]
        rows.append(pl.multiple_of(z1 * 128 + y * 64, 64))
        spot = pl.ds(aligned(y, 64), 64), pl.ds(pl.multiple_of(whole + z1 * HD, HD), HD)
        parts.append([mine[pl.ds(rows[n], 64)], pairs[spot]])
    for row in rows:
        parts.append([att_x[pl.ds(row, 64)], att_x[pl.ds(256 + row, 64)]])
    attended = jnp.concatenate([jnp.concatenate(both, axis=1) for both in parts], axis=0)
    turned = attended.T
    d = None if first else before[...]
    for other in (1, 0):
        c = 1 - at["c"] if other else at["c"]
        for start, tile in tiles:
            cot = jnp.concatenate(
                [
                    block[row : row + 64, pl.ds(pl.multiple_of(c * half + start + skip, 128), tile)]
                    for block, row in blocks
                    for half in [block.shape[1] // 2]
                    for skip in [low if half > width else 0]
                ],
                axis=0,
            )
            share = dot(turned, cot, ((1,), (0,)))
            if other:
                give[:, start : start + tile] = share.astype(BF16)
            else:
                keep[:, start : start + tile] = share
            w = jnp.concatenate(
                [ref[:, low + start : low + start + tile] for ref in w_refs[2 * other :][:2]], axis=0
            )
            part = dot(cot, w, ((1,), (1,)))
            d = part if d is None else d + part
    if not last:
        d_refs[0][...] = d
    else:
        for n, row in enumerate(rows):
            for g in range(2):
                share = d[(4 * g + n) * 64 : (4 * g + n + 1) * 64]
                d_refs[g][pl.ds(row, 64)] = share[:, :HD].astype(d_refs[g].dtype)
                d_refs[2 + g][pl.ds(row, 64)] = share[:, HD:].astype(BF16)


def products(limits, blocks, w_all, att, token, before, last):
    low, high = limits
    width = high - low
    outs = [((2 * HD, width), F32), ((2 * HD, width), BF16)]
    if last:
        outs += [((256, HD), F32)] + [((256, HD), BF16)] * 3
    else:
        outs += [((512, 2 * HD), F32)]
    arrays, places = [], []
    for array, row in blocks:
        known = [n for n, other in enumerate(arrays) if other is array]
        places.append((known[0] if known else len(arrays), row))
        if not known:
            arrays.append(array)
    ins = [token, *arrays, *w_all, *att] + ([] if before is None else [before])
    kernel = functools.partial(products_kernel, low, high, before is None, last, places)
    return call("products", kernel, outs, ins, LARGE)


def fence_kernel(token, out):
    out[...] = token[...]


def fence(token, *others, cost):
    token = after(token, *others)
    return call("fence", fence_kernel, [(token.shape, token.dtype)], [token], cost)[0]


def finish_kernel(limits, *refs):
    out = refs[-1]
    for n, (low, high) in enumerate(limits):
        total, pair = refs[1 + 2 * n], refs[2 + 2 * n]
        out[:, low:high] = (total[:HD] + pair[...].astype(F32)).astype(BF16)


def finish(token, limits, totals, pairs):
    ins = [token, *(ref for both in zip(totals, pairs) for ref in both)]
    outs = [((HD, limits[-1][1]), BF16)]
    return call("finish", functools.partial(finish_kernel, limits), outs, ins, LAST)[0]


def after(value, *others):
    return lax.optimization_barrier((value, *others))[0]


def two(a, b):
    return jnp.concatenate([a, b])


def cut(value, cuts):
    half = value.shape[1] // 2
    return [
        jnp.concatenate([value[:, low:high], value[:, half + low : half + high]], axis=1)
        for low, high in cuts
    ]


def after(value, *others):
    return lax.optimization_barrier((value, *others))[0]


CUTS = ((0, 768), (768, 1536))


def on_device_4x8(queries, keys, values, w_out, cotangent):
    m, o, token = pack(cotangent, ((0, CUTS[-1][1]),))
    probs, mine, bundle = forward(queries, keys, values, w_out)
    ya = send(m, y=1)
    pair_w = send(after(bundle, ya), z0=1)
    x = send(o, x=1)
    yx = send(after(x, x), y=1)
    core_pair_w = send(after(pair_w, yx), c=1)
    at0 = fence(token, core_pair_w, cost=20000000000)
    x1, x2 = cut(x, CUTS)
    zb1 = send(x1, z1=1)
    sb1 = send(after(zb1, zb1), y=1)
    whole = w_out.shape[1]
    att = jnp.concatenate([mine, pair_w[:, whole : whole + HD], pair_w[:, whole + HD :]])
    att_x = send(after(att, ya), x=1)
    own = mine
    za = send(m, z1=1)
    sa = send(za, y=1)
    zb2 = send(after(x2, yx), z1=1)
    sb2 = send(zb2, y=1)
    core_w = send(after(w_out, pair_w), c=1)
    w_all = [w_out, pair_w, core_w, core_pair_w]
    own = after(mine, yx, sa, core_pair_w)
    blocks = [(m, 0), (ya, 0), (za, 0), (sa, 0), (x, 0), (yx, 0), (zb1, 0), (sb1, 0)]
    keep1, give1, d = products(
        CUTS[0], blocks, w_all, [own, att_x], token, None, False
    )
    blocks = [(m, 0), (ya, 0), (za, 0), (sa, 0), (x, 0), (yx, 0), (zb2, 0), (sb2, 0)]
    keep2, give2, d, to_x, to_z, to_xz = products(
        CUTS[1], blocks, w_all, [own, att_x], token, d, True
    )
    got1 = send(after(give1, att_x, zb1, give1), c=1)
    total1 = keep1 + got1.astype(F32)
    to_pair1 = total1[HD:].astype(BF16)
    got2 = send(after(give2, to_pair1, sb1), c=1)
    at1 = fence(at0, sb1, got2, cost=1)
    at2 = fence(at1, zb1, to_pair1, cost=20000000000)
    pair1 = send(after(to_pair1, to_pair1), z0=1)
    queries = after(queries, pair1)
    from_x = send(to_x, x=1)
    from_z = send(after(to_z, give1), z0=1)
    from_xz = send(to_xz, x=1, z0=1)
    *grads, end = backward(
        at2, queries, keys, values, probs, d, from_x, from_z, from_xz
    )
    total2 = keep2 + got2.astype(F32)
    to_pair2 = total2[HD:].astype(BF16)
    pair2 = send(to_pair2, z0=1)
    totals, pairs = [total1, total2], [pair1, pair2]
    return *grads, finish(token, CUTS, totals, pairs)


def solution(mesh):
    in_specs = (P("dp", "mp"), P("dp", "mp"), P("dp", "mp"), P("mp", "dp"), P(("dp", "mp"), None))
    out_specs = (P("dp", "mp"), P("dp", "mp"), P("dp", "mp"), P("mp", "dp"))
    small = mesh.shape["dp"] == 4 and mesh.shape["mp"] == 8
    return jax.shard_map(
        on_device_4x8 if small else on_device,
        mesh=mesh,
        in_specs=in_specs,
        out_specs=out_specs,
        check_vma=False,
    )
```

```python
import functools

import jax
import jax.numpy as jnp
from jax import lax
from jax.experimental import pallas as pl
from jax.experimental.pallas import tpu as pltpu
from jax.sharding import PartitionSpec as P

HD = 128
PATCH = 256
AXES = ("dp", "mp")
ANY = pl.BlockSpec(memory_space=pl.ANY)
VMEM = pl.BlockSpec(memory_space=pltpu.VMEM)
F32 = jnp.float32
SMALL, LARGE, LAST = 10000000000, 10000000000, 20000000000
BF16 = jnp.bfloat16


def forward_attention(queries, keys, values):
    images = queries.shape[0] // PATCH
    heads_here = queries.shape[1] // HD
    shape_four = (images, PATCH, heads_here, HD)
    scale = HD ** (-0.5)
    query_four = queries.reshape(shape_four)
    key_four = keys.reshape(shape_four)
    value_four = values.reshape(shape_four)
    scores = (
        jnp.einsum("iqhd,ikhd->ihqk", query_four, key_four, preferred_element_type=jnp.float32)
        * scale
    )
    attention = jax.nn.softmax(scores, axis=-1)
    rounded = attention.astype(jnp.bfloat16)
    attended = jnp.einsum(
        "ihqk,ikhd->iqhd", rounded, value_four, preferred_element_type=jnp.float32
    ).astype(jnp.bfloat16)
    return (attended.reshape(queries.shape), attention, rounded)


def backward_attention(queries, keys, values, d_att, attention, rounded):
    images = queries.shape[0] // PATCH
    heads_here = queries.shape[1] // HD
    shape_four = (images, PATCH, heads_here, HD)
    scale = HD ** (-0.5)
    query_four = queries.reshape(shape_four)
    key_four = keys.reshape(shape_four)
    value_four = values.reshape(shape_four)
    grad_four = d_att.reshape(shape_four)
    dprob = jnp.einsum("iqhd,ikhd->ihqk", grad_four, value_four, preferred_element_type=jnp.float32)
    delta = jnp.sum(attention * dprob, axis=-1, keepdims=True)
    dscore = (attention * (dprob - delta) * scale).astype(jnp.bfloat16)
    grad_q = jnp.einsum(
        "ihqk,ikhd->iqhd", dscore, key_four, preferred_element_type=jnp.float32
    ).astype(jnp.bfloat16)
    grad_k = jnp.einsum(
        "ihqk,iqhd->ikhd", dscore, query_four, preferred_element_type=jnp.float32
    ).astype(jnp.bfloat16)
    grad_v = jnp.einsum(
        "ihqk,iqhd->ikhd", rounded, grad_four, preferred_element_type=jnp.float32
    ).astype(jnp.bfloat16)
    return (
        grad_q.reshape(queries.shape),
        grad_k.reshape(queries.shape),
        grad_v.reshape(queries.shape),
    )


def on_device(queries, keys, values, w_out, cotangent):
    attended, attention, rounded = forward_attention(queries, keys, values)
    cot_full = lax.all_gather(cotangent, "mp", axis=0, tiled=True)
    d_full = lax.dot_general(
        cot_full,
        lax.all_gather(w_out, "dp", axis=1, tiled=True),
        (((1,), (1,)), ((), ())),
        preferred_element_type=jnp.float32,
    )
    grad_part = lax.dot_general(
        attended, cot_full, (((0,), (0,)), ((), ())), preferred_element_type=jnp.float32
    )
    d_att = d_full.astype(jnp.bfloat16)
    grad_q, grad_k, grad_v = backward_attention(queries, keys, values, d_att, attention, rounded)
    grad_weight = lax.psum_scatter(
        grad_part.astype(jnp.bfloat16), "dp", scatter_dimension=1, tiled=True
    )
    return (grad_q, grad_k, grad_v, grad_weight)


def flip(x=0, c=0, z1=0, z0=0, y=0):
    mask = (x * 2 + c) * 8 + z1 * 4 + z0 * 2 + y
    return [(i, i ^ mask) for i in range(32)]


def send(value, **bits):
    return lax.ppermute(value, AXES, flip(**bits))


def place():
    dp, mp = lax.axis_index("dp"), lax.axis_index("mp")
    return {"x": dp // 2, "c": dp % 2, "z1": mp // 4, "z0": (mp // 2) % 2, "y": mp % 2}


def aligned(index, unit):
    return pl.multiple_of(index * unit, unit)


def call(name, kernel, outs, ins, cost, scratch=(), out_space=VMEM):
    return pl.pallas_call(
        kernel,
        out_shape=[jax.ShapeDtypeStruct(shape, kind) for shape, kind in outs],
        in_specs=[VMEM] * len(ins),
        out_specs=[out_space] * len(outs),
        scratch_shapes=list(scratch),
        cost_estimate=pl.CostEstimate(flops=cost, bytes_accessed=1 << 20, transcendentals=0),
        compiler_params=pltpu.CompilerParams(vmem_limit_bytes=16 << 20),
        name=name,
    )(*(pltpu.with_memory_space_constraint(value, pltpu.VMEM) for value in ins))


def pack_kernel(cuts, cot, *outs):
    outs, token = outs[:-1], outs[-1]
    token[...] = jnp.zeros_like(token)
    x = place()["x"]
    quarter = cot.shape[1] // 4
    for n, (low, high) in enumerate(cuts):
        width = high - low
        for other in range(2):
            half = 1 - x if other else x
            for c in range(2):
                start = pl.multiple_of(half * (2 * quarter) + (c * quarter + low), 128)
                outs[2 * n + other][:, c * width : (c + 1) * width] = cot[:, pl.ds(start, width)]


def pack(cot, cuts):
    outs = []
    for low, high in cuts:
        outs += [((cot.shape[0], 2 * (high - low)), BF16)] * 2
    outs.append(((8, 128), F32))
    return call("pack", functools.partial(pack_kernel, cuts), outs, [cot], SMALL)


def dot(a, b, over):
    return lax.dot_general(a, b, ((over[0], over[1]), ((), ())), preferred_element_type=F32)


def forward_kernel(q, k, v, w, probs, mine, bundle, held):
    z0 = place()["z0"]
    bundle[:, : w.shape[1]] = w[...]
    half = PATCH // 2
    for i in range(q.shape[0] // PATCH):
        rows = pl.ds(i * PATCH, PATCH)
        scores = dot(k[rows], q[rows], ((1,), (1,))) * (HD**-0.5)
        top = jnp.max(scores, axis=0, keepdims=True)
        raised = jnp.exp(scores - top)
        attention = raised / jnp.sum(raised, axis=0, keepdims=True)
        probs[i] = attention
        held[...] = dot(attention.astype(BF16), v[rows], ((0,), (0,))).astype(BF16)
        mine[pl.ds(i * half, half)] = held[pl.ds(aligned(z0, half), half)]
        bundle[:, w.shape[1] + i * HD : w.shape[1] + (i + 1) * HD] = held[
            pl.ds(aligned(1 - z0, half), half)
        ]


def forward(q, k, v, w):
    images = q.shape[0] // PATCH
    outs = [((images, PATCH, PATCH), F32), ((q.shape[0] // 2, HD), BF16)]
    outs.append(((HD, w.shape[1] + images * HD), BF16))
    scratch = [pltpu.VMEM((PATCH, HD), BF16)]
    return call("forward", forward_kernel, outs, [q, k, v, w], SMALL, scratch)


def backward_kernel(at, q, k, v, probs, own, from_x, from_z, from_xz, gq, gk, gv, end, held):
    end[...] = at[...]
    z0 = place()["z0"]
    half = PATCH // 2
    mine = (own[...] + from_x[...].astype(F32)).astype(BF16)
    others = (from_z[...].astype(F32) + from_xz[...].astype(F32)).astype(BF16)
    for i in range(q.shape[0] // PATCH):
        held[i, pl.ds(aligned(z0, half), half)] = mine[i * half : (i + 1) * half]
        held[i, pl.ds(aligned(1 - z0, half), half)] = others[i * half : (i + 1) * half]
    for i in range(q.shape[0] // PATCH):
        rows = pl.ds(i * PATCH, PATCH)
        attention, d_att = probs[i], held[i]
        dprob = dot(v[rows], d_att, ((1,), (1,)))
        delta = jnp.sum(attention * dprob, axis=0, keepdims=True)
        dscore = (attention * (dprob - delta) * (HD**-0.5)).astype(BF16)
        gv[rows] = dot(attention.astype(BF16), d_att, ((1,), (0,))).astype(BF16)
        gk[rows] = dot(dscore, q[rows], ((1,), (0,))).astype(BF16)
        gq[rows] = dot(dscore, k[rows], ((0,), (0,))).astype(BF16)


def backward(at, q, k, v, probs, own, from_x, from_z, from_xz):
    images = q.shape[0] // PATCH
    ins = [at, q, k, v, probs, own, from_x, from_z, from_xz]
    scratch = [pltpu.VMEM((images, PATCH, HD), BF16)]
    outs = [(q.shape, BF16)] * 3 + [(at.shape, at.dtype)]
    return call("backward", backward_kernel, outs, ins, LAST, scratch)


def products_kernel(low, high, first, last, places, *refs):
    refs = list(refs[1:])
    arrays = [refs.pop(0) for _ in range(1 + max(array for array, _ in places))]
    blocks = [(arrays[array], row) for array, row in places]
    w_refs = [refs.pop(0) for _ in range(4)]
    mine, att_x = refs.pop(0), refs.pop(0)
    pairs = w_refs[1]
    before = None if first else refs.pop(0)
    keep, give = refs.pop(0), refs.pop(0)
    d_refs = refs
    at = place()
    whole = w_refs[0].shape[1]
    width = high - low
    tiles = [(start, min(768, width - start)) for start in range(0, width, 768)]
    rows, parts = [], []
    for n in range(4):
        z1 = 1 - at["z1"] if n // 2 else at["z1"]
        y = 1 - at["y"] if n % 2 else at["y"]
        rows.append(pl.multiple_of(z1 * 128 + y * 64, 64))
        spot = pl.ds(aligned(y, 64), 64), pl.ds(pl.multiple_of(whole + z1 * HD, HD), HD)
        parts.append([mine[pl.ds(rows[n], 64)], pairs[spot]])
    for row in rows:
        parts.append([att_x[pl.ds(row, 64)], att_x[pl.ds(256 + row, 64)]])
    attended = jnp.concatenate([jnp.concatenate(both, axis=1) for both in parts], axis=0)
    turned = attended.T
    d = None if first else before[...]
    for other in (1, 0):
        c = 1 - at["c"] if other else at["c"]
        for start, tile in tiles:
            cot = jnp.concatenate(
                [
                    block[row : row + 64, pl.ds(pl.multiple_of(c * half + start + skip, 128), tile)]
                    for block, row in blocks
                    for half in [block.shape[1] // 2]
                    for skip in [low if half > width else 0]
                ],
                axis=0,
            )
            share = dot(turned, cot, ((1,), (0,)))
            if other:
                give[:, start : start + tile] = share.astype(BF16)
            else:
                keep[:, start : start + tile] = share
            w = jnp.concatenate(
                [ref[:, low + start : low + start + tile] for ref in w_refs[2 * other :][:2]], axis=0
            )
            part = dot(cot, w, ((1,), (1,)))
            d = part if d is None else d + part
    if not last:
        d_refs[0][...] = d
    else:
        for n, row in enumerate(rows):
            for g in range(2):
                share = d[(4 * g + n) * 64 : (4 * g + n + 1) * 64]
                d_refs[g][pl.ds(row, 64)] = share[:, :HD].astype(d_refs[g].dtype)
                d_refs[2 + g][pl.ds(row, 64)] = share[:, HD:].astype(BF16)


def products(limits, blocks, w_all, att, token, before, last):
    low, high = limits
    width = high - low
    outs = [((2 * HD, width), F32), ((2 * HD, width), BF16)]
    if last:
        outs += [((256, HD), F32)] + [((256, HD), BF16)] * 3
    else:
        outs += [((512, 2 * HD), F32)]
    arrays, places = [], []
    for array, row in blocks:
        known = [n for n, other in enumerate(arrays) if other is array]
        places.append((known[0] if known else len(arrays), row))
        if not known:
            arrays.append(array)
    ins = [token, *arrays, *w_all, *att] + ([] if before is None else [before])
    kernel = functools.partial(products_kernel, low, high, before is None, last, places)
    return call("products", kernel, outs, ins, LARGE)


def fence_kernel(token, out):
    out[...] = token[...]


def fence(token, *others, cost):
    token = after(token, *others)
    return call("fence", fence_kernel, [(token.shape, token.dtype)], [token], cost)[0]


def finish_kernel(limits, *refs):
    out, held, sems = refs[-3:]
    copies = []
    for n, (low, high) in enumerate(limits):
        total, pair = refs[1 + 2 * n], refs[2 + 2 * n]
        held[:, low:high] = (total[:HD] + pair[...].astype(F32)).astype(BF16)
        columns = pl.ds(low, high - low)
        copies.append(
            pltpu.make_async_copy(held.at[:, columns], out.at[:, columns], sems.at[n])
        )
        copies[-1].start()
    for copy in copies:
        copy.wait()


def finish(token, limits, totals, pairs):
    ins = [token, *(ref for both in zip(totals, pairs) for ref in both)]
    whole = (HD, limits[-1][1])
    scratch = [pltpu.VMEM(whole, BF16), pltpu.SemaphoreType.DMA((len(limits),))]
    kernel = functools.partial(finish_kernel, limits)
    return call("finish", kernel, [(whole, BF16)], ins, LAST, scratch, ANY)[0]


def after(value, *others):
    return lax.optimization_barrier((value, *others))[0]


def two(a, b):
    return jnp.concatenate([a, b])


def cut(value, cuts):
    half = value.shape[1] // 2
    return [
        jnp.concatenate([value[:, low:high], value[:, half + low : half + high]], axis=1)
        for low, high in cuts
    ]


def after(value, *others):
    return lax.optimization_barrier((value, *others))[0]


CUTS = ((0, 768), (768, 1536))


def on_device_4x8(queries, keys, values, w_out, cotangent):
    m, o, token = pack(cotangent, ((0, CUTS[-1][1]),))
    probs, mine, bundle = forward(queries, keys, values, w_out)
    ya = send(m, y=1)
    pair_w = send(after(bundle, ya), z0=1)
    x = send(o, x=1)
    yx = send(after(x, x), y=1)
    core_pair_w = send(after(pair_w, yx), c=1)
    at0 = fence(token, core_pair_w, cost=20000000000)
    x1, x2 = cut(x, CUTS)
    zb1 = send(x1, z1=1)
    sb1 = send(after(zb1, zb1), y=1)
    whole = w_out.shape[1]
    att = jnp.concatenate([mine, pair_w[:, whole : whole + HD], pair_w[:, whole + HD :]])
    att_x = send(after(att, ya), x=1)
    own = mine
    za = send(m, z1=1)
    sa = send(za, y=1)
    zb2 = send(after(x2, yx), z1=1)
    sb2 = send(zb2, y=1)
    core_w = send(after(w_out, pair_w), c=1)
    w_all = [w_out, pair_w, core_w, core_pair_w]
    own = after(mine, yx, sa, core_pair_w)
    blocks = [(m, 0), (ya, 0), (za, 0), (sa, 0), (x, 0), (yx, 0), (zb1, 0), (sb1, 0)]
    keep1, give1, d = products(
        CUTS[0], blocks, w_all, [own, att_x], token, None, False
    )
    blocks = [(m, 0), (ya, 0), (za, 0), (sa, 0), (x, 0), (yx, 0), (zb2, 0), (sb2, 0)]
    keep2, give2, d, to_x, to_z, to_xz = products(
        CUTS[1], blocks, w_all, [own, att_x], token, d, True
    )
    got1 = send(after(give1, att_x, zb1, give1), c=1)
    total1 = keep1 + got1.astype(F32)
    to_pair1 = total1[HD:].astype(BF16)
    got2 = send(after(give2, to_pair1, sb1), c=1)
    at1 = fence(at0, sb1, got2, cost=1)
    at2 = fence(at1, zb1, to_pair1, cost=20000000000)
    pair1 = send(after(to_pair1, to_pair1), z0=1)
    queries = after(queries, pair1)
    from_x = send(to_x, x=1)
    from_z = send(after(to_z, give1), z0=1)
    from_xz = send(to_xz, x=1, z0=1)
    *grads, end = backward(
        at2, queries, keys, values, probs, d, from_x, from_z, from_xz
    )
    total2 = keep2 + got2.astype(F32)
    to_pair2 = total2[HD:].astype(BF16)
    pair2 = send(to_pair2, z0=1)
    totals, pairs = [total1, total2], [pair1, pair2]
    return *grads, finish(token, CUTS, totals, pairs)


def solution(mesh):
    in_specs = (P("dp", "mp"), P("dp", "mp"), P("dp", "mp"), P("mp", "dp"), P(("dp", "mp"), None))
    out_specs = (P("dp", "mp"), P("dp", "mp"), P("dp", "mp"), P("mp", "dp"))
    small = mesh.shape["dp"] == 4 and mesh.shape["mp"] == 8
    return jax.shard_map(
        on_device_4x8 if small else on_device,
        mesh=mesh,
        in_specs=in_specs,
        out_specs=out_specs,
        check_vma=False,
    )
```
